32 devices in a mesh: grp: 2 (over y), row: 16 (over z, x, core).
Axes of the slice: x: 2, y: 2, z: 4, core: 2. Of those that a mesh axis runs over, the one named last changes fastest.
Arguments:
- homolog_embedding: bfloat16 [32, 256, 256], P(None, ('grp', 'row')), parts along dimension 1, may hold values from -6 to 6
- presence_indicator: int32 [32, 256], P(None, ('grp', 'row')), parts along dimension 1, may hold values 0 or 1
- former_projection_matrix: bfloat16 [256, 32], replicated, may hold values from -0.375 to 0.375
- latter_projection_matrix: bfloat16 [256, 32], replicated, may hold values from -0.375 to 0.375
- final_projection_matrix: bfloat16 [1024, 128], replicated, may hold values from -1 to 1
- offset_vector: float32 [128], replicated, may hold values from -3 to 3
- couple_increment_cotangent: bfloat16 [256, 128, 128], P(('grp', 'row')), parts along dimension 0, may hold values from -6 to 6
Outputs:
- couple_increment: bfloat16 [256, 128, 128], P(('grp', 'row')), parts along dimension 0
- homolog_embedding_derivative: bfloat16 [32, 256, 256], P(None, ('grp', 'row')), parts along dimension 1
- former_projection_derivative: float32 [512, 32], P('grp'), parts along dimension 0
- latter_projection_derivative: float32 [512, 32], P('grp'), parts along dimension 0
- final_projection_derivative: float32 [2048, 128], P('grp'), parts along dimension 0
- offset_vector_derivative: float32 [256], P('grp'), parts along dimension 0
The draws below stay inside these ranges and needn't reach their ends.
There are 2 independent parts, one for each index of `grp`. The reference program is written for one: setup_inputs(seed, part) draws one part's arguments, and reference() takes and returns one part's arrays. A program takes and returns all parts, laid end to end along the dimension named above; an argument that names none is the same for every part. Nothing has to cross between parts.
All inputs are finite; a program needn't handle non-finite values. No bound on the sum of `presence_indicator` on one device may be relied on, other than what follows from the above.
Results may differ from the reference program's by a relative error of at most 0.0073.
Values may be sent and summed in bfloat16 or wider, within the bound.
No kernel may reach another device: no remote copies, remote signals or barrier semaphores. Data moves between devices by JAX's collectives and lax.ppermute only.
A program may use at most 128 MiB of HBM per device.

```python
import math
import jax
import jax.numpy as jnp
from jax import lax

FEATURE_DEPTH = 256
PROJ_WIDTH = 32
CZ = 128
SLICE_HOMOLOGS = 32
AMINO_TOTAL = 128


def plant(values, own_key, least, top_value):
    longest = values.shape.index(max(values.shape))
    spots = []
    for shift in (0, 1):
        where = [jax.random.randint(jax.random.fold_in(own_key, axis), (), 0, length) for axis, length in enumerate(values.shape)]
        where[longest] = (where[longest] + shift) % values.shape[longest]
        spots.append(tuple(where))
    return values.at[spots[0]].set(least).at[spots[1]].set(top_value)


def level_of(rng, dims, shards, smallest, top_value):
    loudness, own = 1.0, jax.random.fold_in(rng, 6)
    for axis_at, parts in shards:
        draws = jnp.exp(jax.random.uniform(jax.random.fold_in(own, axis_at), (parts,), jnp.float32, smallest / len(shards), top_value / len(shards)))
        loudness = loudness * jnp.repeat(draws, dims[axis_at] // parts).reshape([-1 if axis == axis_at else 1 for axis in range(len(dims))])
    return loudness


def gaussian(key, shape, spread, limit, split=(), kind=jnp.bfloat16):
    drawn = jax.random.normal(key, shape, jnp.float32) * spread
    if len(split) > 0:
        drawn = level_of(key, shape, split, -0.22, 0.18) * drawn
    return jnp.clip(drawn, min=-limit, max=limit).astype(kind)


def setup_inputs(seed: int = 0, part: int = 0) -> dict:
    splits = jax.random.split(jax.random.key(seed), 8)
    own_keys = jax.random.split(jax.random.fold_in(splits[7], part), 8)
    return {
        "homolog_embedding": gaussian(own_keys[0], (SLICE_HOMOLOGS, AMINO_TOTAL, FEATURE_DEPTH), 1.0, 6.0, ((1, 16),)),
        "presence_indicator": plant((jax.random.randint(own_keys[1], (SLICE_HOMOLOGS, AMINO_TOTAL), 0, 8) < 7).astype(jnp.int32), jax.random.fold_in(own_keys[1], 1), 0, 1),
        "former_projection_matrix": gaussian(splits[2], (FEATURE_DEPTH, PROJ_WIDTH), FEATURE_DEPTH ** -0.5, 0.375),
        "latter_projection_matrix": gaussian(splits[3], (FEATURE_DEPTH, PROJ_WIDTH), FEATURE_DEPTH ** -0.5, 0.375),
        "final_projection_matrix": gaussian(splits[4], (PROJ_WIDTH * PROJ_WIDTH, CZ), PROJ_WIDTH ** -0.5, 1.0),
        "offset_vector": gaussian(splits[5], (CZ,), 0.5, 3.0, (), jnp.float32),
        "couple_increment_cotangent": gaussian(own_keys[6], (AMINO_TOTAL, AMINO_TOTAL, CZ), 1.0, 6.0, ((0, 16),)),
    }


def reference(homolog_embedding, presence_indicator, former_projection_matrix, latter_projection_matrix, final_projection_matrix, offset_vector, couple_increment_cotangent):
    standard_precision_type = jnp.float32
    reduced_precision_type = jnp.bfloat16
    collected_source = homolog_embedding.astype(standard_precision_type)
    mean_val = lax.optimization_barrier(jnp.mean(collected_source, axis=-1, keepdims=True))
    centred = collected_source - mean_val
    var_val = lax.optimization_barrier(jnp.mean(centred * centred, axis=-1, keepdims=True))
    reciprocal_spread = lax.rsqrt(var_val + 1e-05)
    standardized_source = centred * reciprocal_spread
    standardized_reduced = standardized_source.astype(reduced_precision_type)
    mask_float = presence_indicator.astype(standard_precision_type)
    linear_scaled_matrix = standardized_reduced.reshape(SLICE_HOMOLOGS * AMINO_TOTAL, FEATURE_DEPTH)
    left = (mask_float[..., None] * jnp.dot(linear_scaled_matrix, former_projection_matrix, preferred_element_type=standard_precision_type).reshape(SLICE_HOMOLOGS, AMINO_TOTAL, PROJ_WIDTH)).astype(reduced_precision_type)
    right = (mask_float[..., None] * jnp.dot(linear_scaled_matrix, latter_projection_matrix, preferred_element_type=standard_precision_type).reshape(SLICE_HOMOLOGS, AMINO_TOTAL, PROJ_WIDTH)).astype(reduced_precision_type)
    left_f = lax.optimization_barrier(left).astype(standard_precision_type)
    right_f = lax.optimization_barrier(right).astype(standard_precision_type)
    counts = jnp.dot(mask_float.T, mask_float) + 1.0
    block = math.gcd(AMINO_TOTAL, 32)
    nblock = AMINO_TOTAL // block

    def step(carry, index):
        d_acc, right_acc = carry
        start = (index * block).astype(jnp.int32)
        left_blk = lax.dynamic_slice_in_dim(left_f, start, block, 1)
        cnt = lax.dynamic_slice_in_dim(counts, start, block, 0)
        outer_sum = jnp.einsum('sic,sje->ijce', left_blk, right_f)
        outer = (outer_sum / cnt[:, :, None, None]).astype(reduced_precision_type).reshape(block * AMINO_TOTAL, PROJ_WIDTH * PROJ_WIDTH)
        update = (jnp.dot(outer, final_projection_matrix, preferred_element_type=standard_precision_type) + offset_vector).astype(reduced_precision_type)
        cot = lax.dynamic_slice_in_dim(couple_increment_cotangent, start, block, 0).reshape(block * AMINO_TOTAL, CZ)
        d_acc = d_acc + jnp.dot(outer.T, cot, preferred_element_type=standard_precision_type)
        d_o = jnp.dot(cot, final_projection_matrix.T, preferred_element_type=standard_precision_type)
        scaled = (d_o.reshape(block, AMINO_TOTAL, PROJ_WIDTH, PROJ_WIDTH) / cnt[:, :, None, None]).astype(reduced_precision_type)
        scaled_f = lax.optimization_barrier(scaled).astype(standard_precision_type)
        left_part = jnp.einsum('ijce,sje->sic', scaled_f, right_f)
        right_acc = right_acc + jnp.einsum('ijce,sic->sje', scaled_f, left_blk)
        return ((d_acc, right_acc), (update.reshape(block, AMINO_TOTAL, CZ), left_part))
    init = (jnp.zeros((PROJ_WIDTH * PROJ_WIDTH, CZ), standard_precision_type), jnp.zeros((SLICE_HOMOLOGS, AMINO_TOTAL, PROJ_WIDTH), standard_precision_type))
    (d_acc, right_acc), (updates, left_parts) = lax.scan(step, init, jnp.arange(nblock, dtype=jnp.int32))
    couple_increment = updates.reshape(AMINO_TOTAL, AMINO_TOTAL, CZ)
    left_sum = jnp.transpose(left_parts, (1, 0, 2, 3)).reshape(SLICE_HOMOLOGS, AMINO_TOTAL, PROJ_WIDTH)
    left_grad = (mask_float[..., None] * left_sum).astype(reduced_precision_type)
    right_grad = (mask_float[..., None] * right_acc).astype(reduced_precision_type)
    former_projection_derivative = jnp.dot(linear_scaled_matrix.T, left_grad.reshape(SLICE_HOMOLOGS * AMINO_TOTAL, PROJ_WIDTH), preferred_element_type=standard_precision_type) / AMINO_TOTAL
    latter_projection_derivative = jnp.dot(linear_scaled_matrix.T, right_grad.reshape(SLICE_HOMOLOGS * AMINO_TOTAL, PROJ_WIDTH), preferred_element_type=standard_precision_type) / AMINO_TOTAL
    final_projection_derivative = d_acc / AMINO_TOTAL
    offset_vector_derivative = lax.optimization_barrier(jnp.sum(couple_increment_cotangent.astype(standard_precision_type), axis=(0, 1))) / AMINO_TOTAL
    standardized_derivative = jnp.dot(left_grad.reshape(SLICE_HOMOLOGS * AMINO_TOTAL, PROJ_WIDTH), former_projection_matrix.T, preferred_element_type=standard_precision_type)
    standardized_derivative = standardized_derivative + jnp.dot(right_grad.reshape(SLICE_HOMOLOGS * AMINO_TOTAL, PROJ_WIDTH), latter_projection_matrix.T, preferred_element_type=standard_precision_type)
    standardized_derivative = standardized_derivative.reshape(SLICE_HOMOLOGS, AMINO_TOTAL, FEATURE_DEPTH)
    former_factor = lax.optimization_barrier(jnp.mean(standardized_derivative, axis=-1, keepdims=True))
    latter_factor = lax.optimization_barrier(jnp.mean(standardized_derivative * standardized_source, axis=-1, keepdims=True))
    homolog_embedding_derivative = ((standardized_derivative - former_factor - standardized_source * latter_factor) * reciprocal_spread).astype(reduced_precision_type)
    return (couple_increment, homolog_embedding_derivative, former_projection_derivative, latter_projection_derivative, final_projection_derivative, offset_vector_derivative)
```

```python
import functools

import jax
import jax.numpy as jnp
from jax import lax
from jax.experimental import pallas as pl
from jax.experimental.pallas import tpu as pltpu
from jax.sharding import PartitionSpec as P

F32 = jnp.float32
BF16 = jnp.bfloat16
LANES = 128
EPS = 1e-05
VMEM_LIMIT = 40 * 1024 * 1024


def dot(a, b, ca=1, cb=0):
    return lax.dot_general(a, b, (((ca,), (cb,)), ((), ())), preferred_element_type=F32)


def normalize(msa_ref):
    homologs, lines, depth = msa_ref.shape
    x = msa_ref[...].astype(F32).reshape(homologs * lines, depth)
    centred = x - jnp.mean(x, axis=-1, keepdims=True)
    spread = lax.rsqrt(jnp.mean(centred * centred, axis=-1, keepdims=True) + EPS)
    return centred * spread, spread


def pre_kernel(
    msa_ref, mask_ref, wf_ref, wl_ref, cot_ref,
    pay_ref, left_ref, right_ref, maskb_ref, low_ref,
    norm_scr, cot_scr,
):
    homologs, lines, depth = msa_ref.shape
    width = wf_ref.shape[1]
    rows = homologs * lines
    wide = width * homologs
    total, pair_ch = cot_ref.shape[1:]
    normed, _ = normalize(msa_ref)
    for h in range(depth // LANES):
        norm_scr[h] = normed[:, h * LANES : (h + 1) * LANES]
    low = jnp.concatenate(
        [
            jnp.concatenate(
                [norm_scr[h, pl.ds(k, homologs, stride=lines), :] for k in range(lines)], axis=0
            )
            for h in range(depth // LANES)
        ],
        axis=1,
    ).astype(BF16)
    low_ref[...] = low
    mask = mask_ref[...].astype(F32)
    cols = [jnp.broadcast_to(mask[:, k : k + 1], (homologs, LANES)) for k in range(lines)]
    for k in range(lines):
        maskb_ref[:, k * LANES : (k + 1) * LANES] = cols[k].astype(BF16)
    mask_rows = jnp.concatenate(cols, axis=0)
    left = (dot(low, wf_ref[...]) * mask_rows[:, :width]).astype(BF16)
    right = (dot(low, wl_ref[...]) * mask_rows[:, :width]).astype(BF16)
    left_ref[...] = left
    right_ref[...] = right
    spread_to = (
        lax.broadcasted_iota(jnp.int32, (width, wide), 1) // homologs
        == lax.broadcasted_iota(jnp.int32, (width, wide), 0)
    ).astype(BF16)
    own_tile = (
        lax.broadcasted_iota(jnp.int32, (homologs, LANES), 1) % homologs
        == lax.broadcasted_iota(jnp.int32, (homologs, LANES), 0)
    ).astype(F32)
    own_rows = jnp.concatenate([own_tile] * lines, axis=0)
    own = jnp.concatenate([own_rows] * (wide // LANES), axis=1)
    first = (lax.broadcasted_iota(jnp.int32, (rows, LANES), 1) < homologs).astype(F32)
    fold = (
        lax.broadcasted_iota(jnp.int32, (lines, rows), 1) // homologs
        == lax.broadcasted_iota(jnp.int32, (lines, rows), 0)
    ).astype(BF16)
    parts = [
        dot(fold, (dot(right, spread_to) * own).astype(BF16)),
        dot(fold, (dot(left, spread_to) * own).astype(BF16)),
        dot(fold, (mask_rows * own_rows * first).astype(BF16)),
    ]
    same = jnp.concatenate(parts, axis=1)
    same = jnp.concatenate([same, same], axis=0).astype(BF16)
    base = same.shape[1]
    cot_scr[...] = cot_ref[...].astype(F32).reshape(lines * total, pair_ch)
    for pair in range(total // (2 * lines)):
        at = pl.ds(pair * 2 * lines, 2 * lines)
        pay_ref[at, 0:base] = same
        for k in range(lines):
            block = jnp.concatenate(
                [
                    cot_scr[pl.ds((2 * pair + h) * lines + k, lines, stride=total), :]
                    for h in range(2)
                ],
                axis=0,
            )
            pay_ref[at, base + k * pair_ch : base + (k + 1) * pair_ch] = block.astype(BF16)


def mid_kernel(
    half_ref, got_ref, cot_ref, wout_ref, left_ref, right_ref, maskb_ref, low_ref,
    keep_ref, send_ref, grads_ref, inv_ref, wleft_ref,
    w_scr, p_scr, q_scr, half_scr,
):
    lines, total, pair_ch = cot_ref.shape
    homologs = maskb_ref.shape[0]
    width = left_ref.shape[1]
    wide = width * homologs
    rows = lines * homologs
    base = 2 * wide + LANES
    counts = dot(got_ref[:, 2 * wide : 2 * wide + homologs], maskb_ref[...]) + 1.0
    inv = 1.0 / counts
    inv_ref[...] = inv
    by_col = (got_ref[:, base:].astype(F32) * inv).astype(BF16)
    cot = [cot_ref[k].astype(F32) for k in range(lines)]
    by_row = jnp.concatenate(
        [(cot[k] * inv[:, k * LANES : (k + 1) * LANES]).astype(BF16) for k in range(lines)], axis=1
    )
    bias = functools.reduce(jnp.add, [jnp.sum(c, axis=0, keepdims=True) for c in cot])
    w_scr[...] = wout_ref[...].astype(F32)
    for e in range(width):
        wleft_ref[:, e * pair_ch : (e + 1) * pair_ch] = w_scr[
            pl.ds(e, width, stride=width), :
        ].astype(BF16)
    wright = jnp.concatenate(
        [wout_ref[c * width : (c + 1) * width, :] for c in range(width)], axis=1
    )
    group = LANES // homologs

    def contract(source, other, out):
        for g in range(wide // LANES):
            part = dot(source[:, g * LANES : (g + 1) * LANES], other, 0, 0).astype(BF16)
            for b in range(group):
                c = g * group + b
                for k in range(lines):
                    out[k * homologs : (k + 1) * homologs, c * pair_ch : (c + 1) * pair_ch] = part[
                        b * homologs : (b + 1) * homologs, k * pair_ch : (k + 1) * pair_ch
                    ]

    contract(got_ref[:, wide : 2 * wide], by_col, p_scr)
    contract(got_ref[:, 0:wide], by_row, q_scr)
    mask_rows = jnp.concatenate(
        [maskb_ref[:, k * LANES : k * LANES + width] for k in range(lines)], axis=0
    ).astype(F32)
    right_grad = (dot(p_scr[...], wright, 1, 1) * mask_rows).astype(BF16)
    left_grad = (dot(q_scr[...], wleft_ref[...], 1, 1) * mask_rows).astype(BF16)
    grads_ref[0] = left_grad
    grads_ref[1] = right_grad
    d_out = dot(right_ref[...], p_scr[...], 0, 0)
    part_left = dot(left_grad, low_ref[...], 0, 0)
    part_right = dot(right_grad, low_ref[...], 0, 0)
    half = width // 2
    for h in range(2):
        for c in range(half):
            at = (h * half + c) * pair_ch
            half_scr[h, c * width : (c + 1) * width, :] = d_out[:, at : at + pair_ch]
        at = half * width
        depth = low_ref.shape[1] // 2
        half_scr[h, at : at + width, :] = part_left[:, h * depth : (h + 1) * depth]
        half_scr[h, at + width : at + 2 * width, :] = part_right[:, h * depth : (h + 1) * depth]
        half_scr[h, at + 2 * width :, :] = jnp.broadcast_to(
            bias, (half_scr.shape[1] - at - 2 * width, pair_ch)
        )
    me = half_ref[0]
    keep_ref[...] = half_scr[me]
    send_ref[...] = half_scr[1 - me].astype(BF16)


def update_kernel(got_ref, inv_ref, left_ref, wleft_ref, offset_ref, out_ref, lw_scr):
    lines, total, pair_ch = out_ref.shape
    rows, width = left_ref.shape
    homologs = rows // lines
    wide = width * homologs
    for e in range(width):
        part = dot(left_ref[...], wleft_ref[:, e * pair_ch : (e + 1) * pair_ch]).astype(BF16)
        for k in range(lines):
            lw_scr[e * homologs : (e + 1) * homologs, k * pair_ch : (k + 1) * pair_ch] = part[
                k * homologs : (k + 1) * homologs, :
            ]
    update = dot(got_ref[:, 0:wide], lw_scr[...]) * inv_ref[...]
    for k in range(lines):
        out_ref[k] = (update[:, k * pair_ch : (k + 1) * pair_ch] + offset_ref[...]).astype(BF16)


def msa_kernel(msa_ref, grads_ref, wf_ref, wl_ref, out_ref, scr):
    homologs, lines, depth = msa_ref.shape
    derivative = dot(grads_ref[0], wf_ref[...], 1, 1) + dot(grads_ref[1], wl_ref[...], 1, 1)
    for h in range(depth // LANES):
        for k in range(lines):
            scr[h, pl.ds(k, homologs, stride=lines), :] = derivative[
                k * homologs : (k + 1) * homologs, h * LANES : (h + 1) * LANES
            ]
    derivative = jnp.concatenate([scr[h] for h in range(depth // LANES)], axis=1)
    normed, spread = normalize(msa_ref)
    one = jnp.mean(derivative, axis=-1, keepdims=True)
    two = jnp.mean(derivative * normed, axis=-1, keepdims=True)
    out = (derivative - one - normed * two) * spread
    out_ref[...] = out.reshape(homologs, lines, depth).astype(BF16)


def last_kernel(total, half_ref, own_ref, other_ref, out_ref, former_ref, latter_ref, offset_ref):
    me = half_ref[0]
    scale = 1.0 / total
    width = former_ref.shape[1]
    half = out_ref.shape[0] // 2
    own = own_ref[...].astype(F32) * scale
    other = other_ref[...].astype(F32) * scale
    out_ref[pl.ds(pl.multiple_of(me * half, half), half), :] = own[:half]
    out_ref[pl.ds(pl.multiple_of((1 - me) * half, half), half), :] = other[:half]
    own_part, other_part = own[half : half + 2 * width], other[half : half + 2 * width]
    first = me == 0
    both = jnp.concatenate(
        [
            jnp.where(first, own_part, other_part).T,
            jnp.where(first, other_part, own_part).T,
        ],
        axis=0,
    )
    former_ref[...] = both[:, :width]
    latter_ref[...] = both[:, width:]
    offset_ref[...] = own[half + 2 * width : half + 2 * width + 1]


def call(kernel, outs, scratch=(), smem=0, ins=0, flops=0):
    vmem = pl.BlockSpec(memory_space=pltpu.VMEM)
    return pl.pallas_call(
        kernel,
        out_shape=[jax.ShapeDtypeStruct(shape, kind) for shape, kind in outs],
        in_specs=[pl.BlockSpec(memory_space=pltpu.SMEM)] * smem + [vmem] * ins,
        out_specs=[vmem] * len(outs),
        scratch_shapes=[pltpu.VMEM(shape, kind) for shape, kind in scratch],
        compiler_params=pltpu.CompilerParams(vmem_limit_bytes=VMEM_LIMIT),
        cost_estimate=pl.CostEstimate(flops=flops, bytes_accessed=2 * 1024 * 1024, transcendentals=0),
    )


def body(size, msa, mask, wf, wl, wout, offset, cot):
    homologs, lines, depth = msa.shape
    width = wf.shape[1]
    total, pair_ch = cot.shape[1:]
    wide = width * homologs
    rows = lines * homologs
    span = 2 * wide + LANES + lines * pair_ch
    payload, left, right, maskb, low = call(
        pre_kernel,
        [
            ((total, span), BF16),
            ((rows, width), BF16),
            ((rows, width), BF16),
            ((homologs, lines * LANES), BF16),
            ((rows, depth), BF16),
        ],
        [((depth // LANES, rows, LANES), F32), ((lines * total, pair_ch), F32)],
        ins=5,
    )(msa, mask, wf, wl, cot)
    got = lax.all_to_all(payload.reshape(size, lines, span), "row", 0, 0).reshape(total, span)
    me = (lax.axis_index("row") % 2).astype(jnp.int32).reshape(1)
    length = width * width // 2 + 2 * width + 16
    keep, send, grads, inv, wleft = call(
        mid_kernel,
        [
            ((length, pair_ch), F32),
            ((length, pair_ch), BF16),
            ((2, rows, width), BF16),
            ((total, lines * LANES), F32),
            ((width, width * pair_ch), BF16),
        ],
        [
            ((width * width, pair_ch), F32),
            ((rows, width * pair_ch), BF16),
            ((rows, width * pair_ch), BF16),
            ((2, length, pair_ch), F32),
        ],
        smem=1,
        ins=7,
    )(me, got, cot, wout, left, right, maskb, low)

    def swap(x, step):
        return lax.ppermute(x, "row", [(i, i ^ step) for i in range(size)])

    sums = (keep + swap(send, 1).astype(F32)).astype(BF16)
    step = 2
    while step < size:
        sums = (sums.astype(F32) + swap(sums, step).astype(F32)).astype(BF16)
        step *= 2
    others = swap(sums, 1)
    d_out, d_former, d_latter, d_offset = call(
        functools.partial(last_kernel, total),
        [
            ((width * width, pair_ch), F32),
            ((depth, width), F32),
            ((depth, width), F32),
            ((1, pair_ch), F32),
        ],
        smem=1,
        ins=2,
    )(me, sums, others)
    (update,) = call(
        update_kernel,
        [((lines, total, pair_ch), BF16)],
        [((wide, lines * pair_ch), BF16)],
        ins=5,
        flops=2 * total * wide * lines * pair_ch,
    )(got, inv, left, wleft, offset.reshape(1, pair_ch))
    (d_msa,) = call(
        msa_kernel,
        [((homologs, lines, depth), BF16)],
        [((depth // LANES, rows, LANES), F32)],
        ins=4,
        flops=2 * rows * depth * 2 * width,
    )(msa, grads, wf, wl)
    return update, d_msa, d_former, d_latter, d_out, d_offset.reshape(pair_ch)


def solution(mesh):
    return jax.shard_map(
        functools.partial(body, mesh.shape["row"]),
        mesh=mesh,
        in_specs=(
            P(None, ("grp", "row"), None),
            P(None, ("grp", "row")),
            P(),
            P(),
            P(),
            P(),
            P(("grp", "row"), None, None),
        ),
        out_specs=(
            P(("grp", "row"), None, None),
            P(None, ("grp", "row"), None),
            P("grp", None),
            P("grp", None),
            P("grp", None),
            P("grp"),
        ),
        check_vma=False,
    )
```

```python
import functools

import jax
import jax.numpy as jnp
from jax import lax
from jax.experimental import pallas as pl
from jax.experimental.pallas import tpu as pltpu
from jax.sharding import PartitionSpec as P

F32 = jnp.float32
BF16 = jnp.bfloat16
LANES = 128
EPS = 1e-05
VMEM_LIMIT = 40 * 1024 * 1024


def dot(a, b, ca=1, cb=0):
    return lax.dot_general(a, b, (((ca,), (cb,)), ((), ())), preferred_element_type=F32)


def normalize(msa_ref):
    homologs, lines, depth = msa_ref.shape
    x = msa_ref[...].astype(F32).reshape(homologs * lines, depth)
    centred = x - jnp.mean(x, axis=-1, keepdims=True)
    spread = lax.rsqrt(jnp.mean(centred * centred, axis=-1, keepdims=True) + EPS)
    return centred * spread, spread


def pre_kernel(
    half_ref, msa_hbm, mask_hbm, wf_hbm, wl_hbm, cot_hbm,
    pay_ref, cot_out_ref, left_ref, right_ref, maskb_ref, low_ref,
    msa_ref, mask_ref, wf_ref, wl_ref, cot_ref, norm_scr, cot_scr, sems,
):
    copies = [
        pltpu.make_async_copy(source, target, sems.at[n])
        for n, (source, target) in enumerate(
            [
                (msa_hbm, msa_ref),
                (wf_hbm, wf_ref),
                (wl_hbm, wl_ref),
                (mask_hbm, mask_ref),
                (cot_hbm, cot_ref),
            ]
        )
    ]
    for copy in copies:
        copy.start()
    homologs, lines, depth = msa_ref.shape
    width = wf_ref.shape[0]
    rows = homologs * lines
    wide = width * homologs
    total, pair_ch = cot_ref.shape[1:]
    even = half_ref[0] == 0
    copies[0].wait()
    normed, _ = normalize(msa_ref)
    for h in range(depth // LANES):
        norm_scr[h] = normed[:, h * LANES : (h + 1) * LANES]
    low = jnp.concatenate(
        [
            jnp.concatenate(
                [norm_scr[h, pl.ds(k, homologs, stride=lines), :] for k in range(lines)], axis=0
            )
            for h in range(depth // LANES)
        ],
        axis=1,
    ).astype(BF16)
    low_ref[...] = low
    for copy in copies[1:4]:
        copy.wait()
    mask = mask_ref[...].astype(F32).T
    cols = [jnp.broadcast_to(mask[:, k : k + 1], (homologs, LANES)) for k in range(lines)]
    for k in range(lines):
        maskb_ref[:, k * LANES : (k + 1) * LANES] = cols[k].astype(BF16)
    mask_rows = jnp.concatenate(cols, axis=0)
    left = (dot(low, wf_ref[...], 1, 1) * mask_rows[:, :width]).astype(BF16)
    right = (dot(low, wl_ref[...], 1, 1) * mask_rows[:, :width]).astype(BF16)
    left_ref[...] = left
    right_ref[...] = right
    spread_to = (
        lax.broadcasted_iota(jnp.int32, (width, wide), 1) // homologs
        == lax.broadcasted_iota(jnp.int32, (width, wide), 0)
    ).astype(BF16)
    own_tile = (
        lax.broadcasted_iota(jnp.int32, (homologs, LANES), 1) % homologs
        == lax.broadcasted_iota(jnp.int32, (homologs, LANES), 0)
    ).astype(F32)
    own_rows = jnp.concatenate([own_tile] * lines, axis=0)
    own = jnp.concatenate([own_rows] * (wide // LANES), axis=1)
    first = (lax.broadcasted_iota(jnp.int32, (rows, LANES), 1) < homologs).astype(F32)
    fold = (
        lax.broadcasted_iota(jnp.int32, (lines, rows), 1) // homologs
        == lax.broadcasted_iota(jnp.int32, (lines, rows), 0)
    ).astype(BF16)
    same = jnp.concatenate(
        [
            dot(fold, (dot(right, spread_to) * own).astype(BF16)),
            dot(fold, (dot(left, spread_to) * own).astype(BF16)),
            dot(fold, (mask_rows * own_rows * first).astype(BF16)),
        ],
        axis=1,
    )
    same = jnp.concatenate([same, same], axis=0).astype(BF16)
    base = same.shape[1]
    cols = lines * pair_ch
    copies[4].wait()
    cot_scr[...] = cot_ref[...].astype(F32).reshape(lines * total, pair_ch)
    peers = total // (2 * lines)
    for q in range(0, peers, 2):
        at = pl.ds(q * lines, 2 * lines)
        pay_ref[at, cols : cols + base] = same
        for k in range(lines):
            block = [
                [
                    cot_scr[pl.ds((2 * (q + h) + core) * lines + k, lines, stride=total), :]
                    for core in range(2)
                ]
                for h in range(2)
            ]
            mine = jnp.concatenate([jnp.where(even, b[0], b[1]) for b in block], axis=0)
            yours = jnp.concatenate([jnp.where(even, b[1], b[0]) for b in block], axis=0)
            pay_ref[at, k * pair_ch : (k + 1) * pair_ch] = mine.astype(BF16)
            to = cols + base + k * pair_ch
            pay_ref[at, to : to + pair_ch] = yours.astype(BF16)
    for k in range(lines):
        tiles = [
            cot_scr[k * total + n * lines : k * total + (n + 1) * lines, :] for n in range(2 * peers)
        ]
        mine = [jnp.where(even, tiles[2 * q], tiles[2 * q + 1]) for q in range(peers)]
        yours = [jnp.where(even, tiles[2 * q + 1], tiles[2 * q]) for q in range(peers)]
        cot_out_ref[k] = jnp.concatenate(mine + yours, axis=0).astype(BF16)


def mid_kernel(
    half_ref, near_ref, far_ref, cot_ref, wout_ref, left_ref, right_ref, maskb_ref, low_ref,
    keep_ref, send_ref, grads_ref, inv_ref, wleft_ref,
    w_scr, p_scr, q_scr, half_scr,
):
    lines, total, pair_ch = cot_ref.shape
    homologs = maskb_ref.shape[0]
    width = left_ref.shape[1]
    wide = width * homologs
    rows = lines * homologs
    cols = lines * pair_ch
    base = cols + 2 * wide + LANES

    def both(start, size):
        return jnp.concatenate(
            [near_ref[:, start : start + size], far_ref[:, start : start + size]], axis=0
        )

    counts = dot(both(cols + 2 * wide, LANES)[:, :homologs], maskb_ref[...]) + 1.0
    inv = 1.0 / counts
    inv_ref[...] = inv
    by_col = jnp.concatenate([near_ref[:, :cols], far_ref[:, base:]], axis=0)
    by_col = (by_col.astype(F32) * inv).astype(BF16)
    cot = [cot_ref[k].astype(F32) for k in range(lines)]
    by_row = jnp.concatenate(
        [(cot[k] * inv[:, k * LANES : (k + 1) * LANES]).astype(BF16) for k in range(lines)], axis=1
    )
    bias = functools.reduce(jnp.add, [jnp.sum(c, axis=0, keepdims=True) for c in cot])
    w_scr[...] = wout_ref[...].astype(F32)
    for e in range(width):
        wleft_ref[:, e * pair_ch : (e + 1) * pair_ch] = w_scr[
            pl.ds(e, width, stride=width), :
        ].astype(BF16)
    wright = jnp.concatenate(
        [wout_ref[c * width : (c + 1) * width, :] for c in range(width)], axis=1
    )
    group = LANES // homologs

    def contract(source, other, out):
        for g in range(wide // LANES):
            part = dot(source[:, g * LANES : (g + 1) * LANES], other, 0, 0).astype(BF16)
            for b in range(group):
                c = g * group + b
                for k in range(lines):
                    out[k * homologs : (k + 1) * homologs, c * pair_ch : (c + 1) * pair_ch] = part[
                        b * homologs : (b + 1) * homologs, k * pair_ch : (k + 1) * pair_ch
                    ]

    contract(both(cols + wide, wide), by_col, p_scr)
    contract(both(cols, wide), by_row, q_scr)
    mask_rows = jnp.concatenate(
        [maskb_ref[:, k * LANES : k * LANES + width] for k in range(lines)], axis=0
    ).astype(F32)
    right_grad = (dot(p_scr[...], wright, 1, 1) * mask_rows).astype(BF16)
    left_grad = (dot(q_scr[...], wleft_ref[...], 1, 1) * mask_rows).astype(BF16)
    grads_ref[0] = left_grad
    grads_ref[1] = right_grad
    d_out = dot(right_ref[...], p_scr[...], 0, 0)
    part_left = dot(left_grad, low_ref[...], 0, 0)
    part_right = dot(right_grad, low_ref[...], 0, 0)
    half = width // 2
    for h in range(2):
        for c in range(half):
            at = (h * half + c) * pair_ch
            half_scr[h, c * width : (c + 1) * width, :] = d_out[:, at : at + pair_ch]
        at = half * width
        depth = low_ref.shape[1] // 2
        half_scr[h, at : at + width, :] = part_left[:, h * depth : (h + 1) * depth]
        half_scr[h, at + width : at + 2 * width, :] = part_right[:, h * depth : (h + 1) * depth]
        half_scr[h, at + 2 * width :, :] = jnp.broadcast_to(
            bias, (half_scr.shape[1] - at - 2 * width, pair_ch)
        )
    me = half_ref[0]
    keep_ref[...] = half_scr[me]
    send_ref[...] = half_scr[1 - me].astype(BF16)


def update_kernel(
    half_ref, near_ref, far_ref, inv_ref, left_ref, wleft_ref, offset_ref, out_ref, lw_scr
):
    lines, total, pair_ch = out_ref.shape
    cols = lines * pair_ch
    even = half_ref[0] == 0
    rows, width = left_ref.shape
    homologs = rows // lines
    wide = width * homologs
    for e in range(width):
        part = dot(left_ref[...], wleft_ref[:, e * pair_ch : (e + 1) * pair_ch]).astype(BF16)
        for k in range(lines):
            lw_scr[e * homologs : (e + 1) * homologs, k * pair_ch : (k + 1) * pair_ch] = part[
                k * homologs : (k + 1) * homologs, :
            ]
    right = jnp.concatenate(
        [near_ref[:, cols : cols + wide], far_ref[:, cols : cols + wide]], axis=0
    )
    update = dot(right, lw_scr[...]) * inv_ref[...]
    for k in range(lines):
        line = update[:, k * pair_ch : (k + 1) * pair_ch] + offset_ref[...]
        tiles = [line[n * lines : (n + 1) * lines] for n in range(total // lines)]
        near, far = tiles[: len(tiles) // 2], tiles[len(tiles) // 2 :]
        order = []
        for a, b in zip(near, far):
            order += [jnp.where(even, a, b), jnp.where(even, b, a)]
        out_ref[k] = jnp.concatenate(order, axis=0).astype(BF16)


def msa_kernel(msa_ref, grads_ref, wf_ref, wl_ref, out_ref, scr):
    homologs, lines, depth = msa_ref.shape
    derivative = dot(grads_ref[0], wf_ref[...]) + dot(grads_ref[1], wl_ref[...])
    for h in range(depth // LANES):
        for k in range(lines):
            scr[h, pl.ds(k, homologs, stride=lines), :] = derivative[
                k * homologs : (k + 1) * homologs, h * LANES : (h + 1) * LANES
            ]
    derivative = jnp.concatenate([scr[h] for h in range(depth // LANES)], axis=1)
    normed, spread = normalize(msa_ref)
    one = jnp.mean(derivative, axis=-1, keepdims=True)
    two = jnp.mean(derivative * normed, axis=-1, keepdims=True)
    out = (derivative - one - normed * two) * spread
    out_ref[...] = out.reshape(homologs, lines, depth).astype(BF16)


def last_kernel(total, half_ref, own_ref, other_ref, out_ref, former_ref, latter_ref, offset_ref):
    me = half_ref[0]
    scale = 1.0 / total
    width = former_ref.shape[0]
    half = out_ref.shape[0] // 2
    own = own_ref[...].astype(F32) * scale
    other = other_ref[...].astype(F32) * scale
    out_ref[pl.ds(pl.multiple_of(me * half, half), half), :] = own[:half]
    out_ref[pl.ds(pl.multiple_of((1 - me) * half, half), half), :] = other[:half]
    own_part, other_part = own[half : half + 2 * width], other[half : half + 2 * width]
    first = me == 0
    both = jnp.concatenate(
        [jnp.where(first, own_part, other_part), jnp.where(first, other_part, own_part)], axis=1
    )
    former_ref[...] = both[:width]
    latter_ref[...] = both[width:]
    offset_ref[...] = own[half + 2 * width : half + 2 * width + 1]


def call(kernel, outs, scratch=(), smem=0, ins=0, flops=0, away=0, limit=VMEM_LIMIT):
    vmem = pl.BlockSpec(memory_space=pltpu.VMEM)
    return pl.pallas_call(
        kernel,
        out_shape=[jax.ShapeDtypeStruct(shape, kind) for shape, kind in outs],
        in_specs=[pl.BlockSpec(memory_space=pltpu.SMEM)] * smem
        + [pl.BlockSpec(memory_space=pltpu.HBM)] * away
        + [vmem] * ins,
        out_specs=[vmem] * len(outs),
        scratch_shapes=[pltpu.VMEM(shape, kind) for shape, kind in scratch]
        + [pltpu.SemaphoreType.DMA((away,))] * (away > 0),
        compiler_params=pltpu.CompilerParams(vmem_limit_bytes=limit),
        cost_estimate=pl.CostEstimate(flops=flops, bytes_accessed=2 * 1024 * 1024, transcendentals=0),
    )


def body(size, msa, mask, wf, wl, wout, offset, cot):
    homologs, lines, depth = msa.shape
    width = wf.shape[1]
    total, pair_ch = cot.shape[1:]
    wide = width * homologs
    rows = lines * homologs
    cols = lines * pair_ch
    span = 2 * wide + LANES + 2 * cols
    wf, wl = wf.T, wl.T
    me = (lax.axis_index("row") % 2).astype(jnp.int32).reshape(1)
    given = [msa, mask.T, wf, wl, cot]
    payload, cot, left, right, maskb, low = call(
        pre_kernel,
        [
            ((total // 2, span), BF16),
            ((lines, total, pair_ch), BF16),
            ((rows, width), BF16),
            ((rows, width), BF16),
            ((homologs, lines * LANES), BF16),
            ((rows, depth), BF16),
        ],
        [(x.shape, x.dtype) for x in given]
        + [((depth // LANES, rows, LANES), F32), ((lines * total, pair_ch), F32)],
        smem=1,
        away=len(given),
        limit=None,
    )(me, *given)

    def swap(x, step):
        return lax.ppermute(x, "row", [(i, i ^ step) for i in range(size)])

    near = lax.all_to_all(
        payload.reshape(size // 2, lines, span),
        "row",
        0,
        0,
        axis_index_groups=[list(range(core, size, 2)) for core in range(2)],
    ).reshape(total // 2, span)
    far = swap(near, 1)
    length = width * width // 2 + 2 * width + 16
    keep, send, grads, inv, wleft = call(
        mid_kernel,
        [
            ((length, pair_ch), F32),
            ((length, pair_ch), BF16),
            ((2, rows, width), BF16),
            ((total, lines * LANES), F32),
            ((width, width * pair_ch), BF16),
        ],
        [
            ((width * width, pair_ch), F32),
            ((rows, width * pair_ch), BF16),
            ((rows, width * pair_ch), BF16),
            ((2, length, pair_ch), F32),
        ],
        smem=1,
        ins=8,
    )(me, near, far, cot, wout, left, right, maskb, low)

    def add(x, y):
        return (x.astype(F32) + y.astype(F32)).astype(BF16)

    def make_update():
        (out,) = call(
            update_kernel,
            [((lines, total, pair_ch), BF16)],
            [((wide, cols), BF16)],
            smem=1,
            ins=6,
            flops=2 * total * wide * cols,
        )(me, near, far, inv, left, wleft, offset.reshape(1, pair_ch))
        return out

    def make_d_msa():
        (out,) = call(
            msa_kernel,
            [((homologs, lines, depth), BF16)],
            [((depth // LANES, rows, LANES), F32)],
            ins=4,
            flops=2 * rows * depth * 2 * width,
        )(msa, grads, wf, wl)
        return out

    work = [make_d_msa, make_update]
    done = []
    sums = add(keep, swap(send, 1))
    step = 2
    while step < size:
        got = swap(sums, step)
        if work:
            out = work.pop(0)()
            got, out = lax.optimization_barrier((got, out))
            done.append(out)
        sums = add(sums, got)
        step *= 2
    done += [make() for make in work]
    d_msa, update = done
    others = swap(sums, 1)
    d_out, d_former, d_latter, d_offset = call(
        functools.partial(last_kernel, total),
        [
            ((width * width, pair_ch), F32),
            ((width, depth), F32),
            ((width, depth), F32),
            ((1, pair_ch), F32),
        ],
        smem=1,
        ins=2,
    )(me, sums, others)
    return update, d_msa, d_former.T, d_latter.T, d_out, d_offset.reshape(pair_ch)


def solution(mesh):
    return jax.shard_map(
        functools.partial(body, mesh.shape["row"]),
        mesh=mesh,
        in_specs=(
            P(None, ("grp", "row"), None),
            P(None, ("grp", "row")),
            P(),
            P(),
            P(),
            P(),
            P(("grp", "row"), None, None),
        ),
        out_specs=(
            P(("grp", "row"), None, None),
            P(None, ("grp", "row"), None),
            P("grp", None),
            P("grp", None),
            P("grp", None),
            P("grp"),
        ),
        check_vma=False,
    )
```

```python
import functools

import jax
import jax.numpy as jnp
from jax import lax
from jax.experimental import pallas as pl
from jax.experimental.pallas import tpu as pltpu
from jax.sharding import PartitionSpec as P

F32 = jnp.float32
BF16 = jnp.bfloat16
LANES = 128
EPS = 1e-05
VMEM_LIMIT = 40 * 1024 * 1024


def dot(a, b, ca=1, cb=0):
    return lax.dot_general(a, b, (((ca,), (cb,)), ((), ())), preferred_element_type=F32)


def normalize(msa_ref):
    homologs, lines, depth = msa_ref.shape
    x = msa_ref[...].astype(F32).reshape(homologs * lines, depth)
    centred = x - jnp.mean(x, axis=-1, keepdims=True)
    spread = lax.rsqrt(jnp.mean(centred * centred, axis=-1, keepdims=True) + EPS)
    return centred * spread, spread


def pre_kernel(
    half_ref, msa_hbm, mask_hbm, wf_hbm, wl_hbm, cot_hbm,
    pay_ref, cot_out_ref, left_ref, right_ref, maskb_ref, low_ref,
    msa_ref, mask_ref, wf_ref, wl_ref, cot_ref, norm_scr, cot_scr, sems,
):
    copies = [
        pltpu.make_async_copy(source, target, sems.at[n])
        for n, (source, target) in enumerate(
            [
                (msa_hbm, msa_ref),
                (wf_hbm, wf_ref),
                (wl_hbm, wl_ref),
                (mask_hbm, mask_ref),
                (cot_hbm, cot_ref),
            ]
        )
    ]
    for copy in copies:
        copy.start()
    homologs, lines, depth = msa_ref.shape
    width = wf_ref.shape[0]
    rows = homologs * lines
    wide = width * homologs
    total, pair_ch = cot_ref.shape[1:]
    even = half_ref[0] == 0
    copies[0].wait()
    normed, _ = normalize(msa_ref)
    for h in range(depth // LANES):
        norm_scr[h] = normed[:, h * LANES : (h + 1) * LANES]
    low = jnp.concatenate(
        [
            jnp.concatenate(
                [norm_scr[h, pl.ds(k, homologs, stride=lines), :] for k in range(lines)], axis=0
            )
            for h in range(depth // LANES)
        ],
        axis=1,
    ).astype(BF16)
    low_ref[...] = low
    for copy in copies[1:4]:
        copy.wait()
    mask = mask_ref[...].astype(F32).T
    cols = [jnp.broadcast_to(mask[:, k : k + 1], (homologs, LANES)) for k in range(lines)]
    for k in range(lines):
        maskb_ref[:, k * LANES : (k + 1) * LANES] = cols[k].astype(BF16)
    mask_rows = jnp.concatenate(cols, axis=0)
    left = (dot(low, wf_ref[...], 1, 1) * mask_rows[:, :width]).astype(BF16)
    right = (dot(low, wl_ref[...], 1, 1) * mask_rows[:, :width]).astype(BF16)
    left_ref[...] = left
    right_ref[...] = right
    spread_to = (
        lax.broadcasted_iota(jnp.int32, (width, wide), 1) // homologs
        == lax.broadcasted_iota(jnp.int32, (width, wide), 0)
    ).astype(BF16)
    own_tile = (
        lax.broadcasted_iota(jnp.int32, (homologs, LANES), 1) % homologs
        == lax.broadcasted_iota(jnp.int32, (homologs, LANES), 0)
    ).astype(F32)
    own_rows = jnp.concatenate([own_tile] * lines, axis=0)
    own = jnp.concatenate([own_rows] * (wide // LANES), axis=1)
    first = (lax.broadcasted_iota(jnp.int32, (rows, LANES), 1) < homologs).astype(F32)
    fold = (
        lax.broadcasted_iota(jnp.int32, (lines, rows), 1) // homologs
        == lax.broadcasted_iota(jnp.int32, (lines, rows), 0)
    ).astype(BF16)
    same = jnp.concatenate(
        [
            dot(fold, (dot(right, spread_to) * own).astype(BF16)),
            dot(fold, (dot(left, spread_to) * own).astype(BF16)),
            dot(fold, (mask_rows * own_rows * first).astype(BF16)),
        ],
        axis=1,
    )
    same = jnp.concatenate([same, same], axis=0).astype(BF16)
    base = same.shape[1]
    cols = lines * pair_ch
    copies[4].wait()
    cot_scr[...] = cot_ref[...].astype(F32).reshape(lines * total, pair_ch)
    peers = total // (2 * lines)
    for q in range(0, peers, 2):
        at = pl.ds(q * lines, 2 * lines)
        pay_ref[at, cols : cols + base] = same
        for k in range(lines):
            block = [
                [
                    cot_scr[pl.ds((2 * (q + h) + core) * lines + k, lines, stride=total), :]
                    for core in range(2)
                ]
                for h in range(2)
            ]
            mine = jnp.concatenate([jnp.where(even, b[0], b[1]) for b in block], axis=0)
            yours = jnp.concatenate([jnp.where(even, b[1], b[0]) for b in block], axis=0)
            pay_ref[at, k * pair_ch : (k + 1) * pair_ch] = mine.astype(BF16)
            to = cols + base + k * pair_ch
            pay_ref[at, to : to + pair_ch] = yours.astype(BF16)
    for k in range(lines):
        tiles = [
            cot_scr[k * total + n * lines : k * total + (n + 1) * lines, :] for n in range(2 * peers)
        ]
        mine = [jnp.where(even, tiles[2 * q], tiles[2 * q + 1]) for q in range(peers)]
        yours = [jnp.where(even, tiles[2 * q + 1], tiles[2 * q]) for q in range(peers)]
        cot_out_ref[k] = jnp.concatenate(mine + yours, axis=0).astype(BF16)


def mid_kernel(
    half_ref, near_ref, far_ref, cot_ref, wout_ref, left_ref, right_ref, maskb_ref, low_ref,
    keep_a_ref, keep_b_ref, send_a_ref, send_b_ref, grads_ref, inv_ref, wleft_ref,
    w_scr, p_scr, q_scr, half_scr,
):
    lines, total, pair_ch = cot_ref.shape
    homologs = maskb_ref.shape[0]
    width = left_ref.shape[1]
    wide = width * homologs
    rows = lines * homologs
    cols = lines * pair_ch
    base = cols + 2 * wide + LANES

    def both(start, size):
        return jnp.concatenate(
            [near_ref[:, start : start + size], far_ref[:, start : start + size]], axis=0
        )

    counts = dot(both(cols + 2 * wide, LANES)[:, :homologs], maskb_ref[...]) + 1.0
    inv = 1.0 / counts
    inv_ref[...] = inv
    by_col = jnp.concatenate([near_ref[:, :cols], far_ref[:, base:]], axis=0)
    by_col = (by_col.astype(F32) * inv).astype(BF16)
    cot = [cot_ref[k].astype(F32) for k in range(lines)]
    by_row = jnp.concatenate(
        [(cot[k] * inv[:, k * LANES : (k + 1) * LANES]).astype(BF16) for k in range(lines)], axis=1
    )
    bias = functools.reduce(jnp.add, [jnp.sum(c, axis=0, keepdims=True) for c in cot])
    w_scr[...] = wout_ref[...].astype(F32)
    for e in range(width):
        wleft_ref[:, e * pair_ch : (e + 1) * pair_ch] = w_scr[
            pl.ds(e, width, stride=width), :
        ].astype(BF16)
    wright = jnp.concatenate(
        [wout_ref[c * width : (c + 1) * width, :] for c in range(width)], axis=1
    )
    group = LANES // homologs

    def contract(source, other, out):
        for g in range(wide // LANES):
            part = dot(source[:, g * LANES : (g + 1) * LANES], other, 0, 0).astype(BF16)
            for b in range(group):
                c = g * group + b
                for k in range(lines):
                    out[k * homologs : (k + 1) * homologs, c * pair_ch : (c + 1) * pair_ch] = part[
                        b * homologs : (b + 1) * homologs, k * pair_ch : (k + 1) * pair_ch
                    ]

    contract(both(cols + wide, wide), by_col, p_scr)
    contract(both(cols, wide), by_row, q_scr)
    mask_rows = jnp.concatenate(
        [maskb_ref[:, k * LANES : k * LANES + width] for k in range(lines)], axis=0
    ).astype(F32)
    right_grad = (dot(p_scr[...], wright, 1, 1) * mask_rows).astype(BF16)
    left_grad = (dot(q_scr[...], wleft_ref[...], 1, 1) * mask_rows).astype(BF16)
    grads_ref[0] = left_grad
    grads_ref[1] = right_grad
    d_out = dot(right_ref[...], p_scr[...], 0, 0)
    part_left = dot(left_grad, low_ref[...], 0, 0)
    part_right = dot(right_grad, low_ref[...], 0, 0)
    half = width // 2
    for h in range(2):
        for c in range(half):
            at = (h * half + c) * pair_ch
            half_scr[h, c * width : (c + 1) * width, :] = d_out[:, at : at + pair_ch]
        at = half * width
        depth = low_ref.shape[1] // 2
        half_scr[h, at : at + width, :] = part_left[:, h * depth : (h + 1) * depth]
        half_scr[h, at + width : at + 2 * width, :] = part_right[:, h * depth : (h + 1) * depth]
        half_scr[h, at + 2 * width :, :] = jnp.broadcast_to(
            bias, (half_scr.shape[1] - at - 2 * width, pair_ch)
        )
    me = half_ref[0]
    cut = keep_a_ref.shape[0]
    keep_a_ref[...] = half_scr[me, :cut]
    keep_b_ref[...] = half_scr[me, cut:]
    send_a_ref[...] = half_scr[1 - me, :cut].astype(BF16)
    send_b_ref[...] = half_scr[1 - me, cut:].astype(BF16)


def update_kernel(
    half_ref, near_ref, far_ref, inv_ref, left_ref, wleft_ref, offset_ref, out_ref, lw_scr
):
    lines, total, pair_ch = out_ref.shape
    cols = lines * pair_ch
    even = half_ref[0] == 0
    rows, width = left_ref.shape
    homologs = rows // lines
    wide = width * homologs
    for e in range(width):
        part = dot(left_ref[...], wleft_ref[:, e * pair_ch : (e + 1) * pair_ch]).astype(BF16)
        for k in range(lines):
            lw_scr[e * homologs : (e + 1) * homologs, k * pair_ch : (k + 1) * pair_ch] = part[
                k * homologs : (k + 1) * homologs, :
            ]
    right = jnp.concatenate(
        [near_ref[:, cols : cols + wide], far_ref[:, cols : cols + wide]], axis=0
    )
    update = dot(right, lw_scr[...]) * inv_ref[...]
    for k in range(lines):
        line = update[:, k * pair_ch : (k + 1) * pair_ch] + offset_ref[...]
        tiles = [line[n * lines : (n + 1) * lines] for n in range(total // lines)]
        near, far = tiles[: len(tiles) // 2], tiles[len(tiles) // 2 :]
        order = []
        for a, b in zip(near, far):
            order += [jnp.where(even, a, b), jnp.where(even, b, a)]
        out_ref[k] = jnp.concatenate(order, axis=0).astype(BF16)


def msa_kernel(msa_ref, grads_ref, wf_ref, wl_ref, out_ref, scr):
    homologs, lines, depth = msa_ref.shape
    derivative = dot(grads_ref[0], wf_ref[...]) + dot(grads_ref[1], wl_ref[...])
    for h in range(depth // LANES):
        for k in range(lines):
            scr[h, pl.ds(k, homologs, stride=lines), :] = derivative[
                k * homologs : (k + 1) * homologs, h * LANES : (h + 1) * LANES
            ]
    derivative = jnp.concatenate([scr[h] for h in range(depth // LANES)], axis=1)
    normed, spread = normalize(msa_ref)
    one = jnp.mean(derivative, axis=-1, keepdims=True)
    two = jnp.mean(derivative * normed, axis=-1, keepdims=True)
    out = (derivative - one - normed * two) * spread
    out_ref[...] = out.reshape(homologs, lines, depth).astype(BF16)


def last_kernel(
    total, half_ref, own_a_ref, own_b_ref, other_a_ref, other_b_ref,
    out_ref, former_ref, latter_ref, offset_ref,
):
    me = half_ref[0]
    scale = 1.0 / total
    width = former_ref.shape[0]
    half = out_ref.shape[0] // 2
    own = jnp.concatenate([own_a_ref[...], own_b_ref[...]], axis=0).astype(F32) * scale
    other = jnp.concatenate([other_a_ref[...], other_b_ref[...]], axis=0).astype(F32) * scale
    out_ref[pl.ds(pl.multiple_of(me * half, half), half), :] = own[:half]
    out_ref[pl.ds(pl.multiple_of((1 - me) * half, half), half), :] = other[:half]
    own_part, other_part = own[half : half + 2 * width], other[half : half + 2 * width]
    first = me == 0
    both = jnp.concatenate(
        [jnp.where(first, own_part, other_part), jnp.where(first, other_part, own_part)], axis=1
    )
    former_ref[...] = both[:width]
    latter_ref[...] = both[width:]
    offset_ref[...] = own[half + 2 * width : half + 2 * width + 1]


def call(kernel, outs, scratch=(), smem=0, ins=0, flops=0, away=0, limit=VMEM_LIMIT):
    vmem = pl.BlockSpec(memory_space=pltpu.VMEM)
    return pl.pallas_call(
        kernel,
        out_shape=[jax.ShapeDtypeStruct(shape, kind) for shape, kind in outs],
        in_specs=[pl.BlockSpec(memory_space=pltpu.SMEM)] * smem
        + [pl.BlockSpec(memory_space=pltpu.HBM)] * away
        + [vmem] * ins,
        out_specs=[vmem] * len(outs),
        scratch_shapes=[pltpu.VMEM(shape, kind) for shape, kind in scratch]
        + [pltpu.SemaphoreType.DMA((away,))] * (away > 0),
        compiler_params=pltpu.CompilerParams(vmem_limit_bytes=limit),
        cost_estimate=pl.CostEstimate(flops=flops, bytes_accessed=2 * 1024 * 1024, transcendentals=0),
    )


def body(size, msa, mask, wf, wl, wout, offset, cot):
    homologs, lines, depth = msa.shape
    width = wf.shape[1]
    total, pair_ch = cot.shape[1:]
    wide = width * homologs
    rows = lines * homologs
    cols = lines * pair_ch
    span = 2 * wide + LANES + 2 * cols
    wf, wl = wf.T, wl.T
    me = (lax.axis_index("row") % 2).astype(jnp.int32).reshape(1)
    given = [msa, mask.T, wf, wl, cot]
    payload, cot, left, right, maskb, low = call(
        pre_kernel,
        [
            ((total // 2, span), BF16),
            ((lines, total, pair_ch), BF16),
            ((rows, width), BF16),
            ((rows, width), BF16),
            ((homologs, lines * LANES), BF16),
            ((rows, depth), BF16),
        ],
        [(x.shape, x.dtype) for x in given]
        + [((depth // LANES, rows, LANES), F32), ((lines * total, pair_ch), F32)],
        smem=1,
        away=len(given),
        limit=None,
    )(me, *given)

    def swap(x, step):
        return lax.ppermute(x, "row", [(i, i ^ step) for i in range(size)])

    near = lax.all_to_all(
        payload.reshape(size // 2, lines, span),
        "row",
        0,
        0,
        axis_index_groups=[list(range(core, size, 2)) for core in range(2)],
    ).reshape(total // 2, span)
    far = swap(near, 1)
    length = width * width // 2 + 2 * width + 32
    keep_a, keep_b, send_a, send_b, grads, inv, wleft = call(
        mid_kernel,
        [
            ((length // 2, pair_ch), F32),
            ((length // 2, pair_ch), F32),
            ((length // 2, pair_ch), BF16),
            ((length // 2, pair_ch), BF16),
            ((2, rows, width), BF16),
            ((total, lines * LANES), F32),
            ((width, width * pair_ch), BF16),
        ],
        [
            ((width * width, pair_ch), F32),
            ((rows, width * pair_ch), BF16),
            ((rows, width * pair_ch), BF16),
            ((2, length, pair_ch), F32),
        ],
        smem=1,
        ins=8,
    )(me, near, far, cot, wout, left, right, maskb, low)

    def add(x, y):
        return (x.astype(F32) + y.astype(F32)).astype(BF16)

    def make_update():
        (out,) = call(
            update_kernel,
            [((lines, total, pair_ch), BF16)],
            [((wide, cols), BF16)],
            smem=1,
            ins=6,
            flops=2 * total * wide * cols,
        )(me, near, far, inv, left, wleft, offset.reshape(1, pair_ch))
        return out

    def make_d_msa():
        (out,) = call(
            msa_kernel,
            [((homologs, lines, depth), BF16)],
            [((depth // LANES, rows, LANES), F32)],
            ins=4,
            flops=2 * rows * depth * 2 * width,
        )(msa, grads, wf, wl)
        return out

    work = [make_d_msa, make_update]
    done = []
    steps = [1 << n for n in range(1, size.bit_length() - 1)]
    sums_a, sums_b = add(keep_a, swap(send_a, 1)), add(keep_b, swap(send_b, 1))
    for step_a, step_b in zip(steps, steps[1:] + steps[:1]):
        got_a, got_b = swap(sums_a, step_a), swap(sums_b, step_b)
        if work:
            out = work.pop(0)()
            got_a, got_b, out = lax.optimization_barrier((got_a, got_b, out))
            done.append(out)
        sums_a, sums_b = add(sums_a, got_a), add(sums_b, got_b)
    done += [make() for make in work]
    d_msa, update = done
    d_out, d_former, d_latter, d_offset = call(
        functools.partial(last_kernel, total),
        [
            ((width * width, pair_ch), F32),
            ((width, depth), F32),
            ((width, depth), F32),
            ((1, pair_ch), F32),
        ],
        smem=1,
        ins=4,
    )(me, sums_a, sums_b, swap(sums_a, 1), swap(sums_b, 1))
    return update, d_msa, d_former.T, d_latter.T, d_out, d_offset.reshape(pair_ch)


def solution(mesh):
    return jax.shard_map(
        functools.partial(body, mesh.shape["row"]),
        mesh=mesh,
        in_specs=(
            P(None, ("grp", "row"), None),
            P(None, ("grp", "row")),
            P(),
            P(),
            P(),
            P(),
            P(("grp", "row"), None, None),
        ),
        out_specs=(
            P(("grp", "row"), None, None),
            P(None, ("grp", "row"), None),
            P("grp", None),
            P("grp", None),
            P("grp", None),
            P("grp"),
        ),
        check_vma=False,
    )
```

```python
import functools

import jax
import jax.numpy as jnp
from jax import lax
from jax.experimental import pallas as pl
from jax.experimental.pallas import tpu as pltpu
from jax.sharding import Mesh
from jax.sharding import PartitionSpec as P

F32 = jnp.float32
BF16 = jnp.bfloat16
LANES = 128
EPS = 1e-05
VMEM_LIMIT = 40 * 1024 * 1024
PAIR = 2
DIRECT = 8


def dot(a, b, ca=1, cb=0):
    return lax.dot_general(a, b, (((ca,), (cb,)), ((), ())), preferred_element_type=F32)


def normalize(msa_ref):
    homologs, lines, depth = msa_ref.shape
    x = msa_ref[...].astype(F32).reshape(homologs * lines, depth)
    centred = x - jnp.mean(x, axis=-1, keepdims=True)
    spread = lax.rsqrt(jnp.mean(centred * centred, axis=-1, keepdims=True) + EPS)
    return centred * spread, spread


def pre_kernel(
    pos_ref, msa_hbm, mask_hbm, wf_hbm, wl_hbm, cot_hbm,
    left_ref, right_ref, maskb_ref, low_ref, *refs
):
    slots = refs[:-8]
    msa_ref, mask_ref, wf_ref, wl_ref, cot_ref, norm_scr, cot_scr, sems = refs[-8:]
    copies = [
        pltpu.make_async_copy(source, target, sems.at[n])
        for n, (source, target) in enumerate(
            [
                (msa_hbm, msa_ref),
                (wf_hbm, wf_ref),
                (wl_hbm, wl_ref),
                (mask_hbm, mask_ref),
                (cot_hbm, cot_ref),
            ]
        )
    ]
    for copy in copies:
        copy.start()
    homologs, lines, depth = msa_ref.shape
    width = wf_ref.shape[0]
    rows = homologs * lines
    wide = width * homologs
    total, pair_ch = cot_ref.shape[1:]
    chip, core = pos_ref[0] // 2, pos_ref[0] % 2
    copies[0].wait()
    normed, _ = normalize(msa_ref)
    for h in range(depth // LANES):
        norm_scr[h] = normed[:, h * LANES : (h + 1) * LANES]
    low = jnp.concatenate(
        [
            jnp.concatenate(
                [norm_scr[h, pl.ds(k, homologs, stride=lines), :] for k in range(lines)], axis=0
            )
            for h in range(depth // LANES)
        ],
        axis=1,
    ).astype(BF16)
    low_ref[...] = low
    for copy in copies[1:4]:
        copy.wait()
    mask = mask_ref[...].astype(F32).T
    cols = [jnp.broadcast_to(mask[:, k : k + 1], (homologs, LANES)) for k in range(lines)]
    for k in range(lines):
        maskb_ref[:, k * LANES : (k + 1) * LANES] = cols[k].astype(BF16)
    mask_rows = jnp.concatenate(cols, axis=0)
    left = (dot(low, wf_ref[...], 1, 1) * mask_rows[:, :width]).astype(BF16)
    right = (dot(low, wl_ref[...], 1, 1) * mask_rows[:, :width]).astype(BF16)
    left_ref[...] = left
    right_ref[...] = right
    spread_to = (
        lax.broadcasted_iota(jnp.int32, (width, wide), 1) // homologs
        == lax.broadcasted_iota(jnp.int32, (width, wide), 0)
    ).astype(BF16)
    own_tile = (
        lax.broadcasted_iota(jnp.int32, (homologs, LANES), 1) % homologs
        == lax.broadcasted_iota(jnp.int32, (homologs, LANES), 0)
    ).astype(F32)
    own_rows = jnp.concatenate([own_tile] * lines, axis=0)
    own = jnp.concatenate([own_rows] * (wide // LANES), axis=1)
    first = (lax.broadcasted_iota(jnp.int32, (rows, LANES), 1) < homologs).astype(F32)
    fold = (
        lax.broadcasted_iota(jnp.int32, (lines, rows), 1) // homologs
        == lax.broadcasted_iota(jnp.int32, (lines, rows), 0)
    ).astype(BF16)
    same = jnp.concatenate(
        [
            dot(fold, (dot(right, spread_to) * own).astype(BF16)),
            dot(fold, (dot(left, spread_to) * own).astype(BF16)),
            dot(fold, (mask_rows * own_rows * first).astype(BF16)),
        ],
        axis=1,
    )
    same = same.astype(BF16)
    base = same.shape[1]
    cols = lines * pair_ch
    copies[4].wait()
    cot_scr[...] = cot_ref[...].astype(F32).reshape(lines * total, pair_ch)
    for m, slot in enumerate(slots):
        slot[:, cols : cols + base] = same
        for begin, to in ((0, core), (cols + base, 1 - core)):
            first = (2 * (chip ^ m) + to) * lines
            for k in range(lines):
                slot[:, begin + k * pair_ch : begin + (k + 1) * pair_ch] = cot_scr[
                    pl.ds(first + k, lines, stride=total), :
                ].astype(BF16)


def weight_kernel(wout_ref, wleft_ref, w_scr):
    width, pair_ch = wleft_ref.shape[0], wout_ref.shape[1]
    w_scr[...] = wout_ref[...].astype(F32)
    for e in range(width):
        wleft_ref[:, e * pair_ch : (e + 1) * pair_ch] = w_scr[
            pl.ds(e, width, stride=width), :
        ].astype(BF16)


def half_kernel(offsets, pos_ref, mask_a_ref, mask_b_ref, right_a_ref, right_b_ref, *refs):
    early_ref, late_ref, right_ref, left_ref, by_col_ref, inv_ref, got_scr, p_scr = refs[-8:]
    slots = refs[:-8]
    near, far = slots[: len(slots) // 2], slots[len(slots) // 2 :]
    rows, width = right_a_ref.shape
    homologs, cols = mask_a_ref.shape
    wide = width * homologs
    lines = rows // homologs
    pair_ch = cols // lines
    span = wide // PAIR
    base = cols + 2 * wide + LANES
    chip, core = pos_ref[0] // 2, pos_ref[0] % 2
    for m, a_ref, b_ref in zip(offsets, near, far):
        tile = 2 * (chip ^ m)
        got_scr[tile + core] = a_ref[...]
        got_scr[tile + 1 - core, :, cols:base] = b_ref[:, cols:base]
        got_scr[tile + 1 - core, :, :cols] = b_ref[:, base:]
        got_scr[tile + 1 - core, :, base:] = b_ref[:, :cols]

    def load(start, size):
        return got_scr[:, :, pl.ds(start, size)].astype(F32).reshape(-1, size)

    right_ref[...] = load(cols, wide).astype(BF16)
    left_ref[...] = load(cols + wide, wide).astype(BF16)
    left = left_ref[:, pl.ds(pl.multiple_of(core * span, span), span)]
    masks = load(cols + 2 * wide, LANES).astype(BF16)
    group = LANES // homologs
    for m, (mask_ref, start) in enumerate(((mask_a_ref, 0), (mask_b_ref, base))):
        inv = 1.0 / (dot(masks[:, :homologs], mask_ref[...]) + 1.0)
        cot = (load(start, cols) * inv).astype(BF16)
        if m == 0:
            inv_ref[...] = inv
            by_col_ref[...] = cot
        for g in range(span // LANES):
            part = dot(left[:, g * LANES : (g + 1) * LANES], cot, 0, 0).astype(BF16)
            for b in range(group):
                c = g * group + b
                for k in range(lines):
                    to = m * rows + k * homologs
                    p_scr[to : to + homologs, c * pair_ch : (c + 1) * pair_ch] = part[
                        b * homologs : (b + 1) * homologs, k * pair_ch : (k + 1) * pair_ch
                    ]
    right = jnp.concatenate([right_a_ref[...], right_b_ref[...]], axis=0)
    out = dot(right, p_scr[...], 0, 0).astype(BF16)
    cut = early_ref.shape[0] // width
    for c in range(width // PAIR):
        line = out[:, c * pair_ch : (c + 1) * pair_ch]
        if c < cut:
            early_ref[c * width : (c + 1) * width, :] = line
        else:
            late_ref[(c - cut) * width : (c - cut + 1) * width, :] = line


def grads_kernel(
    right_ref, left_ref, by_col_ref, inv_ref, cot_ref, wout_ref, wleft_ref, maskb_ref, low_ref, late_ref,
    parts_ref, grads_ref,
    pq_scr,
):
    lines, total, pair_ch = cot_ref.shape
    homologs = maskb_ref.shape[0]
    width = wleft_ref.shape[0]
    wide = width * homologs
    rows = lines * homologs
    bias = 0.0
    by_row = []
    for k in range(lines):
        line = cot_ref[k].astype(F32)
        bias = bias + jnp.sum(line, axis=0, keepdims=True)
        by_row.append((line * inv_ref[:, k * LANES : (k + 1) * LANES]).astype(BF16))
    by_row = jnp.concatenate(by_row, axis=1)
    group = LANES // homologs
    for first, source, other in (
        (0, left_ref, by_col_ref[...]),
        (rows, right_ref, by_row),
    ):
        for g in range(wide // LANES):
            part = dot(source[:, g * LANES : (g + 1) * LANES], other, 0, 0).astype(BF16)
            for b in range(group):
                c = g * group + b
                for k in range(lines):
                    at = first + k * homologs
                    pq_scr[at : at + homologs, c * pair_ch : (c + 1) * pair_ch] = part[
                        b * homologs : (b + 1) * homologs, k * pair_ch : (k + 1) * pair_ch
                    ]
    wright = jnp.concatenate(
        [wout_ref[c * width : (c + 1) * width, :] for c in range(width)], axis=1
    )
    mask_rows = jnp.concatenate(
        [maskb_ref[:, k * LANES : k * LANES + width] for k in range(lines)], axis=0
    ).astype(F32)
    right_grad = (dot(pq_scr[:rows], wright, 1, 1) * mask_rows).astype(BF16)
    left_grad = (dot(pq_scr[rows:], wleft_ref[...], 1, 1) * mask_rows).astype(BF16)
    grads_ref[0] = left_grad
    grads_ref[1] = right_grad
    part_left = dot(left_grad, low_ref[...], 0, 0)
    part_right = dot(right_grad, low_ref[...], 0, 0)
    begin = late_ref.shape[0]
    parts_ref[:begin, :] = late_ref[...]
    for h in range(2):
        lanes = slice(h * pair_ch, (h + 1) * pair_ch)
        at = begin + 2 * h * width
        parts_ref[at : at + width, :] = part_left[:, lanes].astype(BF16)
        parts_ref[at + width : at + 2 * width, :] = part_right[:, lanes].astype(BF16)
    at = begin + 4 * width
    parts_ref[at:, :] = jnp.broadcast_to(bias, (parts_ref.shape[0] - at, pair_ch)).astype(BF16)


def update_kernel(right_ref, inv_ref, left_ref, wleft_ref, offset_ref, out_ref, lw_scr):
    lines, total, pair_ch = out_ref.shape
    rows, width = left_ref.shape
    homologs = rows // lines
    for e in range(width):
        part = dot(left_ref[...], wleft_ref[:, e * pair_ch : (e + 1) * pair_ch]).astype(BF16)
        for k in range(lines):
            lw_scr[e * homologs : (e + 1) * homologs, k * pair_ch : (k + 1) * pair_ch] = part[
                k * homologs : (k + 1) * homologs, :
            ]
    update = dot(right_ref[...], lw_scr[...]) * inv_ref[...]
    for k in range(lines):
        out_ref[k] = (update[:, k * pair_ch : (k + 1) * pair_ch] + offset_ref[...]).astype(BF16)


def msa_kernel(msa_ref, grads_ref, wf_ref, wl_ref, out_ref, scr):
    homologs, lines, depth = msa_ref.shape
    derivative = dot(grads_ref[0], wf_ref[...]) + dot(grads_ref[1], wl_ref[...])
    for h in range(depth // LANES):
        for k in range(lines):
            scr[h, pl.ds(k, homologs, stride=lines), :] = derivative[
                k * homologs : (k + 1) * homologs, h * LANES : (h + 1) * LANES
            ]
    derivative = jnp.concatenate([scr[h] for h in range(depth // LANES)], axis=1)
    normed, spread = normalize(msa_ref)
    one = jnp.mean(derivative, axis=-1, keepdims=True)
    two = jnp.mean(derivative * normed, axis=-1, keepdims=True)
    out = (derivative - one - normed * two) * spread
    out_ref[...] = out.reshape(homologs, lines, depth).astype(BF16)


def last_kernel(
    total, pos_ref, own_a_ref, other_a_ref, own_b_ref, other_b_ref,
    out_ref, former_ref, latter_ref, offset_ref,
):
    scale = 1.0 / total
    width = former_ref.shape[0]
    half = out_ref.shape[0] // PAIR
    early = own_a_ref.shape[0]
    late = half - early
    me = pos_ref[0] % PAIR
    for core, a_ref, b_ref in ((me, own_a_ref, own_b_ref), (1 - me, other_a_ref, other_b_ref)):
        at = core * half
        out_ref[pl.ds(pl.multiple_of(at, half), early), :] = a_ref[...].astype(F32) * scale
        out_ref[pl.ds(pl.multiple_of(at + early, width), late), :] = (
            b_ref[:late, :].astype(F32) * scale
        )
    parts = (own_b_ref[late:, :].astype(F32) + other_b_ref[late:, :].astype(F32)) * scale
    both = jnp.concatenate([parts[: 2 * width], parts[2 * width : 4 * width]], axis=1)
    former_ref[...] = both[:width]
    latter_ref[...] = both[width:]
    offset_ref[...] = parts[4 * width : 4 * width + 1]


def call(kernel, outs, scratch=(), smem=0, ins=0, flops=0, away=0, limit=VMEM_LIMIT):
    vmem = pl.BlockSpec(memory_space=pltpu.VMEM)
    return pl.pallas_call(
        kernel,
        out_shape=[jax.ShapeDtypeStruct(shape, kind) for shape, kind in outs],
        in_specs=[pl.BlockSpec(memory_space=pltpu.SMEM)] * smem
        + [pl.BlockSpec(memory_space=pltpu.HBM)] * away
        + [vmem] * ins,
        out_specs=[vmem] * len(outs),
        scratch_shapes=[pltpu.VMEM(shape, kind) for shape, kind in scratch]
        + [pltpu.SemaphoreType.DMA((away,))] * (away > 0),
        compiler_params=pltpu.CompilerParams(vmem_limit_bytes=limit),
        cost_estimate=pl.CostEstimate(flops=flops, bytes_accessed=0, transcendentals=0),
    )


def body(size, msa, mask, wf, wl, wout, offset, cot):
    homologs, lines, depth = msa.shape
    width = wf.shape[1]
    total, pair_ch = cot.shape[1:]
    wide = width * homologs
    rows = lines * homologs
    cols = lines * pair_ch
    span = 2 * wide + LANES + 2 * cols
    wf, wl = wf.T, wl.T
    pos = lax.axis_index(("chip", "core")).astype(jnp.int32).reshape(1)
    given = [msa, mask.T, wf, wl, cot]
    chips = size // 2
    left, right, maskb, low, *slots = call(
        pre_kernel,
        [
            ((rows, width), BF16),
            ((rows, width), BF16),
            ((homologs, lines * LANES), BF16),
            ((rows, depth), BF16),
        ]
        + [((lines, span), BF16)] * chips,
        [(x.shape, x.dtype) for x in given]
        + [((depth // LANES, rows, LANES), F32), ((lines * total, pair_ch), F32)],
        smem=1,
        away=len(given),
        limit=None,
    )(pos, *given)

    def swap(x, step):
        return lax.ppermute(x, ("chip", "core"), [(i, i ^ step) for i in range(size)])

    def add(x, y):
        return (x.astype(F32) + y.astype(F32)).astype(BF16)

    offsets = sorted(range(chips), key=lambda m: (-(m // 4), -(m // 2), m))
    if chips <= DIRECT:
        near = [swap(slots[m], 2 * m) if m else slots[0] for m in offsets]
    else:
        order = (pos[0] // 2) ^ jnp.arange(chips)
        near = lax.all_to_all(jnp.stack(slots)[order], "chip", 0, 0)[order]
        near = [near[m] for m in offsets]
    far = [swap(slot, 1) for slot in near]
    other_right, other_maskb = swap(right, 1), swap(maskb, 1)
    (wleft,) = call(
        weight_kernel,
        [((width, width * pair_ch), BF16)],
        [((width * width, pair_ch), F32)],
        ins=1,
    )(wout)
    near, wleft = lax.optimization_barrier((near, wleft))
    half = width * width // PAIR
    early = half * 7 // 8
    sums, late, all_right, all_left, by_col, inv = call(
        functools.partial(half_kernel, offsets),
        [
            ((early, pair_ch), BF16),
            ((half - early, pair_ch), BF16),
            ((total, wide), BF16),
            ((total, wide), BF16),
            ((total, cols), BF16),
            ((total, cols), F32),
        ],
        [((size, lines, span), BF16), ((PAIR * rows, width * pair_ch // PAIR), BF16)],
        smem=1,
        ins=4 + 2 * chips,
    )(pos, maskb, other_maskb, right, other_right, *near, *far)
    parts, grads = call(
        grads_kernel,
        [
            ((half - early + 4 * width + 16, pair_ch), BF16),
            ((2, rows, width), BF16),
        ],
        [((2 * rows, width * pair_ch), BF16)],
        ins=10,
    )(all_right, all_left, by_col, inv, cot, wout, wleft, maskb, low, late)

    def make_update():
        (out,) = call(
            update_kernel,
            [((lines, total, pair_ch), BF16)],
            [((wide, cols), BF16)],
            ins=5,
            flops=2 * total * wide * cols,
        )(all_right, inv, left, wleft, offset.reshape(1, pair_ch))
        return out

    def make_d_msa():
        (out,) = call(
            msa_kernel,
            [((homologs, lines, depth), BF16)],
            [((depth // LANES, rows, LANES), F32)],
            ins=4,
            flops=2 * rows * depth * 2 * width,
        )(msa, grads, wf, wl)
        return out

    steps = [1 << n for n in range(1, size.bit_length() - 1)]
    work = [make_d_msa, make_update]
    done = []
    for step_a, step_b in zip(steps, steps[1:] + steps[:1]):
        sums = add(sums, swap(sums, step_a))
        got = swap(parts, step_b)
        if work:
            out = work.pop(0)()
            got, out = lax.optimization_barrier((got, out))
            done.append(out)
        parts = add(parts, got)
    d_msa, update = done
    d_out, d_former, d_latter, d_offset = call(
        functools.partial(last_kernel, total),
        [
            ((width * width, pair_ch), F32),
            ((width, depth), F32),
            ((width, depth), F32),
            ((1, pair_ch), F32),
        ],
        smem=1,
        ins=4,
    )(pos, sums, swap(sums, 1), parts, swap(parts, 1))
    return update, d_msa, d_former.T, d_latter.T, d_out, d_offset.reshape(pair_ch)


def solution(mesh):
    size = mesh.shape["row"]
    split = Mesh(mesh.devices.reshape(-1, size // 2, 2), ("grp", "chip", "core"))
    whole = ("grp", "chip", "core")
    return jax.shard_map(
        functools.partial(body, size),
        mesh=split,
        in_specs=(P(None, whole, None), P(None, whole), P(), P(), P(), P(), P(whole, None, None)),
        out_specs=(
            P(whole, None, None),
            P(None, whole, None),
            P("grp", None),
            P("grp", None),
            P("grp", None),
            P("grp"),
        ),
        check_vma=False,
    )
```

```python
import functools

import jax
import jax.numpy as jnp
from jax import lax
from jax.experimental import pallas as pl
from jax.experimental.pallas import tpu as pltpu
from jax.sharding import Mesh
from jax.sharding import PartitionSpec as P

F32 = jnp.float32
BF16 = jnp.bfloat16
LANES = 128
EPS = 1e-05
VMEM_LIMIT = 40 * 1024 * 1024
PAIR = 2
DIRECT = 8


def dot(a, b, ca=1, cb=0):
    return lax.dot_general(a, b, (((ca,), (cb,)), ((), ())), preferred_element_type=F32)


def normalize(msa_ref):
    homologs, lines, depth = msa_ref.shape
    x = msa_ref[...].astype(F32).reshape(homologs * lines, depth)
    centred = x - jnp.mean(x, axis=-1, keepdims=True)
    spread = lax.rsqrt(jnp.mean(centred * centred, axis=-1, keepdims=True) + EPS)
    return centred * spread, spread


def pre_kernel(
    pos_ref, msa_hbm, mask_hbm, wf_hbm, wl_hbm, cot_hbm,
    left_ref, right_ref, maskb_ref, low_ref, *refs
):
    slots, refs = refs[:-13], refs[-13:]
    msa_ref, mask_ref, wf_ref, wl_ref, cot_ref, norm_scr, cot_scr = refs[:7]
    left_scr, right_scr, maskb_scr, low_scr, slot_scr, sems = refs[7:]
    sent = []

    def send(source, target):
        sent.append(pltpu.make_async_copy(source, target, sems.at[len(copies) + len(sent)]))
        sent[-1].start()

    copies = [
        pltpu.make_async_copy(source, target, sems.at[n])
        for n, (source, target) in enumerate(
            [
                (msa_hbm, msa_ref),
                (wf_hbm, wf_ref),
                (wl_hbm, wl_ref),
                (mask_hbm, mask_ref),
                (cot_hbm, cot_ref),
            ]
        )
    ]
    for copy in copies:
        copy.start()
    homologs, lines, depth = msa_ref.shape
    width = wf_ref.shape[0]
    rows = homologs * lines
    wide = width * homologs
    total, pair_ch = cot_ref.shape[1:]
    chip, core = pos_ref[0] // 2, pos_ref[0] % 2
    copies[0].wait()
    normed, _ = normalize(msa_ref)
    for h in range(depth // LANES):
        norm_scr[h] = normed[:, h * LANES : (h + 1) * LANES]
    low = jnp.concatenate(
        [
            jnp.concatenate(
                [norm_scr[h, pl.ds(k, homologs, stride=lines), :] for k in range(lines)], axis=0
            )
            for h in range(depth // LANES)
        ],
        axis=1,
    ).astype(BF16)
    low_scr[...] = low
    send(low_scr, low_ref)
    for copy in copies[1:4]:
        copy.wait()
    mask = mask_ref[...].astype(F32).T
    cols = [jnp.broadcast_to(mask[:, k : k + 1], (homologs, LANES)) for k in range(lines)]
    for k in range(lines):
        maskb_scr[:, k * LANES : (k + 1) * LANES] = cols[k].astype(BF16)
    send(maskb_scr, maskb_ref)
    mask_rows = jnp.concatenate(cols, axis=0)
    left = (dot(low, wf_ref[...], 1, 1) * mask_rows[:, :width]).astype(BF16)
    right = (dot(low, wl_ref[...], 1, 1) * mask_rows[:, :width]).astype(BF16)
    left_scr[...] = left
    right_scr[...] = right
    send(left_scr, left_ref)
    send(right_scr, right_ref)
    spread_to = (
        lax.broadcasted_iota(jnp.int32, (width, wide), 1) // homologs
        == lax.broadcasted_iota(jnp.int32, (width, wide), 0)
    ).astype(BF16)
    own_tile = (
        lax.broadcasted_iota(jnp.int32, (homologs, LANES), 1) % homologs
        == lax.broadcasted_iota(jnp.int32, (homologs, LANES), 0)
    ).astype(F32)
    own_rows = jnp.concatenate([own_tile] * lines, axis=0)
    own = jnp.concatenate([own_rows] * (wide // LANES), axis=1)
    first = (lax.broadcasted_iota(jnp.int32, (rows, LANES), 1) < homologs).astype(F32)
    fold = (
        lax.broadcasted_iota(jnp.int32, (lines, rows), 1) // homologs
        == lax.broadcasted_iota(jnp.int32, (lines, rows), 0)
    ).astype(BF16)
    same = jnp.concatenate(
        [
            dot(fold, (dot(right, spread_to) * own).astype(BF16)),
            dot(fold, (dot(left, spread_to) * own).astype(BF16)),
            dot(fold, (mask_rows * own_rows * first).astype(BF16)),
        ],
        axis=1,
    )
    same = same.astype(BF16)
    base = same.shape[1]
    cols = lines * pair_ch
    copies[4].wait()
    cot_scr[...] = cot_ref[...].astype(F32).reshape(lines * total, pair_ch)
    for m, slot in enumerate(slots):
        slot_scr[m, :, cols : cols + base] = same
        for begin, to in ((0, core), (cols + base, 1 - core)):
            first = (2 * (chip ^ m) + to) * lines
            for k in range(lines):
                slot_scr[m, :, begin + k * pair_ch : begin + (k + 1) * pair_ch] = cot_scr[
                    pl.ds(first + k, lines, stride=total), :
                ].astype(BF16)
        send(slot_scr.at[m], slot)
    for copy in sent:
        copy.wait()


def weight_kernel(wout_ref, wleft_ref, w_scr):
    width, pair_ch = wleft_ref.shape[0], wout_ref.shape[1]
    w_scr[...] = wout_ref[...].astype(F32)
    for e in range(width):
        wleft_ref[:, e * pair_ch : (e + 1) * pair_ch] = w_scr[
            pl.ds(e, width, stride=width), :
        ].astype(BF16)


def half_kernel(offsets, pos_ref, *refs):
    early_ref, late_ref, right_ref, left_ref, by_col_ref, inv_ref, p_ref, got_scr, p_scr = refs[-9:]
    slots, (mask_a_ref, mask_b_ref, right_a_ref, right_b_ref) = refs[:-13], refs[-13:-9]
    near, far = slots[: len(slots) // 2], slots[len(slots) // 2 :]
    rows, width = right_a_ref.shape
    homologs, cols = mask_a_ref.shape
    wide = width * homologs
    lines = rows // homologs
    pair_ch = cols // lines
    span = wide // PAIR
    base = cols + 2 * wide + LANES
    chip, core = pos_ref[0] // 2, pos_ref[0] % 2
    for m, a_ref, b_ref in zip(offsets, near, far):
        tile = 2 * (chip ^ m)
        got_scr[tile + core] = a_ref[...]
        got_scr[tile + 1 - core, :, cols:base] = b_ref[:, cols:base]
        got_scr[tile + 1 - core, :, :cols] = b_ref[:, base:]
        got_scr[tile + 1 - core, :, base:] = b_ref[:, :cols]

    def load(start, size):
        return got_scr[:, :, pl.ds(start, size)].astype(F32).reshape(-1, size)

    right_ref[...] = load(cols, wide).astype(BF16)
    left_ref[...] = load(cols + wide, wide).astype(BF16)
    left = left_ref[:, pl.ds(pl.multiple_of(core * span, span), span)]
    masks = load(cols + 2 * wide, LANES).astype(BF16)
    group = LANES // homologs
    sides = (mask_a_ref, right_a_ref, 0, p_ref), (mask_b_ref, right_b_ref, base, p_scr)
    out = 0.0
    for m, (mask_ref, side_ref, start, to_ref) in enumerate(sides):
        inv = 1.0 / (dot(masks[:, :homologs], mask_ref[...]) + 1.0)
        cot = (load(start, cols) * inv).astype(BF16)
        if m == 0:
            inv_ref[...] = inv
            by_col_ref[...] = cot
        for g in range(span // LANES):
            part = dot(left[:, g * LANES : (g + 1) * LANES], cot, 0, 0).astype(BF16)
            for b in range(group):
                c = g * group + b
                for k in range(lines):
                    to = k * homologs
                    to_ref[to : to + homologs, c * pair_ch : (c + 1) * pair_ch] = part[
                        b * homologs : (b + 1) * homologs, k * pair_ch : (k + 1) * pair_ch
                    ]
        out = out + dot(side_ref[...], to_ref[...], 0, 0)
    out = out.astype(BF16)
    cut = early_ref.shape[0] // width
    for c in range(width // PAIR):
        line = out[:, c * pair_ch : (c + 1) * pair_ch]
        if c < cut:
            early_ref[c * width : (c + 1) * width, :] = line
        else:
            late_ref[(c - cut) * width : (c - cut + 1) * width, :] = line


def grads_kernel(
    pos_ref, p_ref, right_ref, left_ref, by_col_ref, inv_ref, cot_ref, wout_ref, wleft_ref, maskb_ref, low_ref, late_ref,
    parts_ref, grads_ref,
    p_scr, q_scr,
):
    lines, total, pair_ch = cot_ref.shape
    homologs = maskb_ref.shape[0]
    width = wleft_ref.shape[0]
    wide = width * homologs
    rows = lines * homologs
    bias = 0.0
    by_row = []
    for k in range(lines):
        line = cot_ref[k].astype(F32)
        bias = bias + jnp.sum(line, axis=0, keepdims=True)
        by_row.append((line * inv_ref[:, k * LANES : (k + 1) * LANES]).astype(BF16))
    by_row = jnp.concatenate(by_row, axis=1)
    group = LANES // homologs
    span = wide // PAIR
    core = pos_ref[0] % PAIR
    for out_ref, source, other in (
        (p_scr, left_ref[:, pl.ds(pl.multiple_of((1 - core) * span, span), span)], by_col_ref[...]),
        (q_scr, right_ref[...], by_row),
    ):
        for g in range(source.shape[1] // LANES):
            part = dot(source[:, g * LANES : (g + 1) * LANES], other, 0, 0).astype(BF16)
            for b in range(group):
                c = g * group + b
                for k in range(lines):
                    at = k * homologs
                    out_ref[at : at + homologs, c * pair_ch : (c + 1) * pair_ch] = part[
                        b * homologs : (b + 1) * homologs, k * pair_ch : (k + 1) * pair_ch
                    ]

    def weights(half):
        size = wout_ref.shape[0] // PAIR
        block = wout_ref[pl.ds(pl.multiple_of(half * size, size), size), :]
        return jnp.concatenate(
            [block[c * width : (c + 1) * width] for c in range(width // PAIR)], axis=1
        )

    mask_rows = jnp.concatenate(
        [maskb_ref[:, k * LANES : k * LANES + width] for k in range(lines)], axis=0
    ).astype(F32)
    right_sum = dot(p_ref[...], weights(core), 1, 1) + dot(p_scr[...], weights(1 - core), 1, 1)
    right_grad = (right_sum * mask_rows).astype(BF16)
    left_grad = (dot(q_scr[...], wleft_ref[...], 1, 1) * mask_rows).astype(BF16)
    grads_ref[0] = left_grad
    grads_ref[1] = right_grad
    part_left = dot(left_grad, low_ref[...], 0, 0)
    part_right = dot(right_grad, low_ref[...], 0, 0)
    begin = late_ref.shape[0]
    parts_ref[:begin, :] = late_ref[...]
    for h in range(2):
        lanes = slice(h * pair_ch, (h + 1) * pair_ch)
        at = begin + 2 * h * width
        parts_ref[at : at + width, :] = part_left[:, lanes].astype(BF16)
        parts_ref[at + width : at + 2 * width, :] = part_right[:, lanes].astype(BF16)
    at = begin + 4 * width
    parts_ref[at:, :] = jnp.broadcast_to(bias, (parts_ref.shape[0] - at, pair_ch)).astype(BF16)


def update_kernel(right_ref, inv_ref, left_ref, wleft_ref, offset_ref, out_ref, lw_scr):
    lines, total, pair_ch = out_ref.shape
    rows, width = left_ref.shape
    homologs = rows // lines
    for e in range(width):
        part = dot(left_ref[...], wleft_ref[:, e * pair_ch : (e + 1) * pair_ch]).astype(BF16)
        for k in range(lines):
            lw_scr[e * homologs : (e + 1) * homologs, k * pair_ch : (k + 1) * pair_ch] = part[
                k * homologs : (k + 1) * homologs, :
            ]
    update = dot(right_ref[...], lw_scr[...]) * inv_ref[...]
    for k in range(lines):
        out_ref[k] = (update[:, k * pair_ch : (k + 1) * pair_ch] + offset_ref[...]).astype(BF16)


def msa_kernel(msa_ref, grads_ref, wf_ref, wl_ref, out_ref, scr):
    homologs, lines, depth = msa_ref.shape
    derivative = dot(grads_ref[0], wf_ref[...]) + dot(grads_ref[1], wl_ref[...])
    for h in range(depth // LANES):
        for k in range(lines):
            scr[h, pl.ds(k, homologs, stride=lines), :] = derivative[
                k * homologs : (k + 1) * homologs, h * LANES : (h + 1) * LANES
            ]
    derivative = jnp.concatenate([scr[h] for h in range(depth // LANES)], axis=1)
    normed, spread = normalize(msa_ref)
    one = jnp.mean(derivative, axis=-1, keepdims=True)
    two = jnp.mean(derivative * normed, axis=-1, keepdims=True)
    out = (derivative - one - normed * two) * spread
    out_ref[...] = out.reshape(homologs, lines, depth).astype(BF16)


def last_kernel(
    total, pos_ref, own_a_ref, other_a_ref, own_b_ref, other_b_ref,
    out_ref, former_ref, latter_ref, offset_ref,
):
    scale = 1.0 / total
    width = former_ref.shape[0]
    half = out_ref.shape[0] // PAIR
    early = own_a_ref.shape[0]
    late = half - early
    me = pos_ref[0] % PAIR
    for core, a_ref, b_ref in ((me, own_a_ref, own_b_ref), (1 - me, other_a_ref, other_b_ref)):
        at = core * half
        out_ref[pl.ds(pl.multiple_of(at, half), early), :] = a_ref[...].astype(F32) * scale
        out_ref[pl.ds(pl.multiple_of(at + early, width), late), :] = (
            b_ref[:late, :].astype(F32) * scale
        )
    parts = (own_b_ref[late:, :].astype(F32) + other_b_ref[late:, :].astype(F32)) * scale
    both = jnp.concatenate([parts[: 2 * width], parts[2 * width : 4 * width]], axis=1)
    former_ref[...] = both[:width]
    latter_ref[...] = both[width:]
    offset_ref[...] = parts[4 * width : 4 * width + 1]


def call(kernel, outs, scratch=(), smem=0, ins=0, flops=0, away=0, limit=VMEM_LIMIT):
    vmem = pl.BlockSpec(memory_space=pltpu.VMEM)
    return pl.pallas_call(
        kernel,
        out_shape=[jax.ShapeDtypeStruct(shape, kind) for shape, kind in outs],
        in_specs=[pl.BlockSpec(memory_space=pltpu.SMEM)] * smem
        + [pl.BlockSpec(memory_space=pltpu.HBM)] * away
        + [vmem] * ins,
        out_specs=[pl.BlockSpec(memory_space=pl.ANY) if away else vmem] * len(outs),
        scratch_shapes=[pltpu.VMEM(shape, kind) for shape, kind in scratch]
        + [pltpu.SemaphoreType.DMA((away + len(outs),))] * (away > 0),
        compiler_params=pltpu.CompilerParams(vmem_limit_bytes=limit),
        cost_estimate=pl.CostEstimate(flops=flops, bytes_accessed=0, transcendentals=0),
    )


def body(size, msa, mask, wf, wl, wout, offset, cot):
    homologs, lines, depth = msa.shape
    width = wf.shape[1]
    total, pair_ch = cot.shape[1:]
    wide = width * homologs
    rows = lines * homologs
    cols = lines * pair_ch
    span = 2 * wide + LANES + 2 * cols
    wf, wl = wf.T, wl.T
    pos = lax.axis_index(("chip", "core")).astype(jnp.int32).reshape(1)
    given = [msa, mask.T, wf, wl, cot]
    chips = size // 2
    left, right, maskb, low, *slots = call(
        pre_kernel,
        [
            ((rows, width), BF16),
            ((rows, width), BF16),
            ((homologs, lines * LANES), BF16),
            ((rows, depth), BF16),
        ]
        + [((lines, span), BF16)] * chips,
        [(x.shape, x.dtype) for x in given]
        + [
            ((depth // LANES, rows, LANES), F32),
            ((lines * total, pair_ch), F32),
            ((rows, width), BF16),
            ((rows, width), BF16),
            ((homologs, lines * LANES), BF16),
            ((rows, depth), BF16),
            ((chips, lines, span), BF16),
        ],
        smem=1,
        away=len(given),
        limit=None,
    )(pos, *given)

    def swap(x, step):
        return lax.ppermute(x, ("chip", "core"), [(i, i ^ step) for i in range(size)])

    def add(x, y):
        return (x.astype(F32) + y.astype(F32)).astype(BF16)

    offsets = sorted(range(chips), key=lambda m: (-(m // 4), -(m // 2), m))
    if chips <= DIRECT:
        near = [swap(slots[m], 2 * m) if m else slots[0] for m in offsets]
    else:
        order = (pos[0] // 2) ^ jnp.arange(chips)
        near = lax.all_to_all(jnp.stack(slots)[order], "chip", 0, 0)[order]
        near = [near[m] for m in offsets]
    far = [swap(slot, 1) for slot in near]
    other_right, other_maskb = swap(right, 1), swap(maskb, 1)
    (wleft,) = call(
        weight_kernel,
        [((width, width * pair_ch), BF16)],
        [((width * width, pair_ch), F32)],
        ins=1,
    )(wout)
    near, wleft = lax.optimization_barrier((near, wleft))
    half = width * width // PAIR
    early = half * 15 // 16
    sums, late, all_right, all_left, by_col, inv, own_p = call(
        functools.partial(half_kernel, offsets),
        [
            ((early, pair_ch), BF16),
            ((half - early, pair_ch), BF16),
            ((total, wide), BF16),
            ((total, wide), BF16),
            ((total, cols), BF16),
            ((total, cols), F32),
            ((rows, width * pair_ch // PAIR), BF16),
        ],
        [((size, lines, span), BF16), ((rows, width * pair_ch // PAIR), BF16)],
        smem=1,
        ins=4 + 2 * chips,
    )(pos, *near, *far, maskb, other_maskb, right, other_right)
    parts, grads = call(
        grads_kernel,
        [
            ((half - early + 4 * width + 16, pair_ch), BF16),
            ((2, rows, width), BF16),
        ],
        [((rows, width * pair_ch // PAIR), BF16), ((rows, width * pair_ch), BF16)],
        smem=1,
        ins=11,
    )(pos, own_p, all_right, all_left, by_col, inv, cot, wout, wleft, maskb, low, late)

    def make_update():
        (out,) = call(
            update_kernel,
            [((lines, total, pair_ch), BF16)],
            [((wide, cols), BF16)],
            ins=5,
            flops=2 * total * wide * cols,
        )(all_right, inv, left, wleft, offset.reshape(1, pair_ch))
        return out

    def make_d_msa():
        (out,) = call(
            msa_kernel,
            [((homologs, lines, depth), BF16)],
            [((depth // LANES, rows, LANES), F32)],
            ins=4,
            flops=2 * rows * depth * 2 * width,
        )(msa, grads, wf, wl)
        return out

    steps = [1 << n for n in range(1, size.bit_length() - 1)]
    work = [make_d_msa, make_update]
    done = []
    for step_a, step_b in zip(steps, steps[1:] + steps[:1]):
        sums = add(sums, swap(sums, step_a))
        got = swap(parts, step_b)
        if work:
            out = work.pop(0)()
            got, out = lax.optimization_barrier((got, out))
            done.append(out)
        parts = add(parts, got)
    d_msa, update = done
    d_out, d_former, d_latter, d_offset = call(
        functools.partial(last_kernel, total),
        [
            ((width * width, pair_ch), F32),
            ((width, depth), F32),
            ((width, depth), F32),
            ((1, pair_ch), F32),
        ],
        smem=1,
        ins=4,
    )(pos, sums, swap(sums, 1), parts, swap(parts, 1))
    return update, d_msa, d_former.T, d_latter.T, d_out, d_offset.reshape(pair_ch)


def solution(mesh):
    size = mesh.shape["row"]
    split = Mesh(mesh.devices.reshape(-1, size // 2, 2), ("grp", "chip", "core"))
    whole = ("grp", "chip", "core")
    return jax.shard_map(
        functools.partial(body, size),
        mesh=split,
        in_specs=(P(None, whole, None), P(None, whole), P(), P(), P(), P(), P(whole, None, None)),
        out_specs=(
            P(whole, None, None),
            P(None, whole, None),
            P("grp", None),
            P("grp", None),
            P("grp", None),
            P("grp"),
        ),
        check_vma=False,
    )
```

```python
import functools

import jax
import jax.numpy as jnp
from jax import lax
from jax.experimental import pallas as pl
from jax.experimental.pallas import tpu as pltpu
from jax.sharding import Mesh
from jax.sharding import PartitionSpec as P

F32 = jnp.float32
BF16 = jnp.bfloat16
LANES = 128
EPS = 1e-05
VMEM_LIMIT = 40 * 1024 * 1024
PAIR = 2
DIRECT = 8


def dot(a, b, ca=1, cb=0):
    return lax.dot_general(a, b, (((ca,), (cb,)), ((), ())), preferred_element_type=F32)


def normalize(msa_ref):
    homologs, lines, depth = msa_ref.shape
    x = msa_ref[...].astype(F32).reshape(homologs * lines, depth)
    centred = x - jnp.mean(x, axis=-1, keepdims=True)
    spread = lax.rsqrt(jnp.mean(centred * centred, axis=-1, keepdims=True) + EPS)
    return centred * spread, spread


def pre_kernel(
    pos_ref, msa_hbm, mask_hbm, wf_hbm, wl_hbm, cot_hbm,
    left_ref, right_ref, maskb_ref, low_ref, *refs
):
    slots, refs = refs[:-13], refs[-13:]
    msa_ref, mask_ref, wf_ref, wl_ref, cot_ref, norm_scr, cot_scr = refs[:7]
    left_scr, right_scr, maskb_scr, low_scr, slot_scr, sems = refs[7:]
    sent = []

    def send(source, target):
        sent.append(pltpu.make_async_copy(source, target, sems.at[len(copies) + len(sent)]))
        sent[-1].start()

    copies = [
        pltpu.make_async_copy(source, target, sems.at[n])
        for n, (source, target) in enumerate(
            [
                (msa_hbm, msa_ref),
                (wf_hbm, wf_ref),
                (wl_hbm, wl_ref),
                (mask_hbm, mask_ref),
                (cot_hbm, cot_ref),
            ]
        )
    ]
    for copy in copies:
        copy.start()
    homologs, lines, depth = msa_ref.shape
    width = wf_ref.shape[0]
    rows = homologs * lines
    wide = width * homologs
    total, pair_ch = cot_ref.shape[1:]
    chip, core = pos_ref[0] // 2, pos_ref[0] % 2
    copies[0].wait()
    normed, _ = normalize(msa_ref)
    for h in range(depth // LANES):
        norm_scr[h] = normed[:, h * LANES : (h + 1) * LANES]
    low = jnp.concatenate(
        [
            jnp.concatenate(
                [norm_scr[h, pl.ds(k, homologs, stride=lines), :] for k in range(lines)], axis=0
            )
            for h in range(depth // LANES)
        ],
        axis=1,
    ).astype(BF16)
    low_scr[...] = low
    send(low_scr, low_ref)
    for copy in copies[1:4]:
        copy.wait()
    mask = mask_ref[...].astype(F32).T
    cols = [jnp.broadcast_to(mask[:, k : k + 1], (homologs, LANES)) for k in range(lines)]
    for k in range(lines):
        maskb_scr[:, k * LANES : (k + 1) * LANES] = cols[k].astype(BF16)
    send(maskb_scr, maskb_ref)
    mask_rows = jnp.concatenate(cols, axis=0)
    weights = jnp.concatenate([wl_ref[...], wf_ref[...]], axis=0)
    both = (dot(low, weights, 1, 1) * mask_rows[:, : 2 * width]).astype(BF16)
    right, left = both[:, :width], both[:, width:]
    left_scr[...] = left
    right_scr[...] = right
    send(left_scr, left_ref)
    send(right_scr, right_ref)
    spread_to = (
        lax.broadcasted_iota(jnp.int32, (2 * width, 2 * wide), 1) // homologs
        == lax.broadcasted_iota(jnp.int32, (2 * width, 2 * wide), 0)
    ).astype(BF16)
    own_tile = (
        lax.broadcasted_iota(jnp.int32, (homologs, LANES), 1) % homologs
        == lax.broadcasted_iota(jnp.int32, (homologs, LANES), 0)
    ).astype(F32)
    own_rows = jnp.concatenate([own_tile] * lines, axis=0)
    own = jnp.concatenate([own_rows] * (2 * wide // LANES), axis=1)
    first = (lax.broadcasted_iota(jnp.int32, (rows, LANES), 1) < homologs).astype(F32)
    fold = (
        lax.broadcasted_iota(jnp.int32, (lines, rows), 1) // homologs
        == lax.broadcasted_iota(jnp.int32, (lines, rows), 0)
    ).astype(BF16)
    same = jnp.concatenate(
        [
            (dot(both, spread_to) * own).astype(BF16),
            (mask_rows * own_rows * first).astype(BF16),
        ],
        axis=1,
    )
    same = dot(fold, same).astype(BF16)
    base = same.shape[1]
    cols = lines * pair_ch
    copies[4].wait()
    cot_scr[...] = cot_ref[...].astype(F32).reshape(lines * total, pair_ch)
    for m, slot in enumerate(slots):
        slot_scr[m, :, cols : cols + base] = same
        for begin, to in ((0, core), (cols + base, 1 - core)):
            first = (2 * (chip ^ m) + to) * lines
            for k in range(lines):
                slot_scr[m, :, begin + k * pair_ch : begin + (k + 1) * pair_ch] = cot_scr[
                    pl.ds(first + k, lines, stride=total), :
                ].astype(BF16)
        send(slot_scr.at[m], slot)
    for copy in sent:
        copy.wait()


def weight_kernel(wout_ref, wleft_ref, w_scr):
    width, pair_ch = wleft_ref.shape[0], wout_ref.shape[1]
    w_scr[...] = wout_ref[...].astype(F32)
    for e in range(width):
        wleft_ref[:, e * pair_ch : (e + 1) * pair_ch] = w_scr[
            pl.ds(e, width, stride=width), :
        ].astype(BF16)


def half_kernel(offsets, pos_ref, *refs):
    early_ref, late_ref, right_ref, left_ref, by_col_ref, inv_ref, p_ref, got_scr, p_scr = refs[-9:]
    slots, (mask_a_ref, mask_b_ref, right_a_ref, right_b_ref) = refs[:-13], refs[-13:-9]
    near, far = slots[: len(slots) // 2], slots[len(slots) // 2 :]
    rows, width = right_a_ref.shape
    homologs, cols = mask_a_ref.shape
    wide = width * homologs
    lines = rows // homologs
    pair_ch = cols // lines
    span = wide // PAIR
    base = cols + 2 * wide + LANES
    chip, core = pos_ref[0] // 2, pos_ref[0] % 2
    for m, a_ref, b_ref in zip(offsets, near, far):
        tile = 2 * (chip ^ m)
        got_scr[tile + core] = a_ref[...]
        got_scr[tile + 1 - core, :, cols:base] = b_ref[:, cols:base]
        got_scr[tile + 1 - core, :, :cols] = b_ref[:, base:]
        got_scr[tile + 1 - core, :, base:] = b_ref[:, :cols]

    def load(start, size):
        return got_scr[:, :, pl.ds(start, size)].astype(F32).reshape(-1, size)

    right_ref[...] = load(cols, wide).astype(BF16)
    left_ref[...] = load(cols + wide, wide).astype(BF16)
    left = left_ref[:, pl.ds(pl.multiple_of(core * span, span), span)]
    masks = load(cols + 2 * wide, LANES).astype(BF16)
    group = LANES // homologs
    sides = (mask_a_ref, right_a_ref, 0, p_ref), (mask_b_ref, right_b_ref, base, p_scr)
    out = 0.0
    for m, (mask_ref, side_ref, start, to_ref) in enumerate(sides):
        inv = 1.0 / (dot(masks[:, :homologs], mask_ref[...]) + 1.0)
        cot = (load(start, cols) * inv).astype(BF16)
        if m == 0:
            inv_ref[...] = inv
            by_col_ref[...] = cot
        for g in range(span // LANES):
            part = dot(left[:, g * LANES : (g + 1) * LANES], cot, 0, 0).astype(BF16)
            for b in range(group):
                c = g * group + b
                for k in range(lines):
                    to = k * homologs
                    to_ref[to : to + homologs, c * pair_ch : (c + 1) * pair_ch] = part[
                        b * homologs : (b + 1) * homologs, k * pair_ch : (k + 1) * pair_ch
                    ]
        out = out + dot(side_ref[...], to_ref[...], 0, 0)
    out = out.astype(BF16)
    cut = early_ref.shape[0] // width
    for c in range(width // PAIR):
        line = out[:, c * pair_ch : (c + 1) * pair_ch]
        if c < cut:
            early_ref[c * width : (c + 1) * width, :] = line
        else:
            late_ref[(c - cut) * width : (c - cut + 1) * width, :] = line


def grads_kernel(
    pos_ref, p_ref, right_ref, left_ref, by_col_ref, inv_ref, cot_ref, wout_ref, wleft_ref, maskb_ref, low_ref, late_ref,
    parts_ref, grads_ref,
    p_scr, q_scr,
):
    lines, total, pair_ch = cot_ref.shape
    homologs = maskb_ref.shape[0]
    width = wleft_ref.shape[0]
    wide = width * homologs
    rows = lines * homologs
    bias = 0.0
    by_row = []
    for k in range(lines):
        line = cot_ref[k].astype(F32)
        bias = bias + jnp.sum(line, axis=0, keepdims=True)
        by_row.append((line * inv_ref[:, k * LANES : (k + 1) * LANES]).astype(BF16))
    by_row = jnp.concatenate(by_row, axis=1)
    group = LANES // homologs
    span = wide // PAIR
    core = pos_ref[0] % PAIR
    for out_ref, source, other in (
        (p_scr, left_ref[:, pl.ds(pl.multiple_of((1 - core) * span, span), span)], by_col_ref[...]),
        (q_scr, right_ref[...], by_row),
    ):
        for g in range(source.shape[1] // LANES):
            part = dot(source[:, g * LANES : (g + 1) * LANES], other, 0, 0).astype(BF16)
            for b in range(group):
                c = g * group + b
                for k in range(lines):
                    at = k * homologs
                    out_ref[at : at + homologs, c * pair_ch : (c + 1) * pair_ch] = part[
                        b * homologs : (b + 1) * homologs, k * pair_ch : (k + 1) * pair_ch
                    ]

    def weights(half):
        size = wout_ref.shape[0] // PAIR
        block = wout_ref[pl.ds(pl.multiple_of(half * size, size), size), :]
        return jnp.concatenate(
            [block[c * width : (c + 1) * width] for c in range(width // PAIR)], axis=1
        )

    mask_rows = jnp.concatenate(
        [maskb_ref[:, k * LANES : k * LANES + width] for k in range(lines)], axis=0
    ).astype(F32)
    right_sum = dot(p_ref[...], weights(core), 1, 1) + dot(p_scr[...], weights(1 - core), 1, 1)
    right_grad = (right_sum * mask_rows).astype(BF16)
    left_grad = (dot(q_scr[...], wleft_ref[...], 1, 1) * mask_rows).astype(BF16)
    grads_ref[0] = left_grad
    grads_ref[1] = right_grad
    part_left = dot(left_grad, low_ref[...], 0, 0)
    part_right = dot(right_grad, low_ref[...], 0, 0)
    begin = late_ref.shape[0]
    parts_ref[:begin, :] = late_ref[...]
    for h in range(2):
        lanes = slice(h * pair_ch, (h + 1) * pair_ch)
        at = begin + 2 * h * width
        parts_ref[at : at + width, :] = part_left[:, lanes].astype(BF16)
        parts_ref[at + width : at + 2 * width, :] = part_right[:, lanes].astype(BF16)
    at = begin + 4 * width
    parts_ref[at:, :] = jnp.broadcast_to(bias, (parts_ref.shape[0] - at, pair_ch)).astype(BF16)


def update_kernel(right_ref, inv_ref, left_ref, wleft_ref, offset_ref, out_ref, lw_scr):
    lines, total, pair_ch = out_ref.shape
    rows, width = left_ref.shape
    homologs = rows // lines
    for e in range(width):
        part = dot(left_ref[...], wleft_ref[:, e * pair_ch : (e + 1) * pair_ch]).astype(BF16)
        for k in range(lines):
            lw_scr[e * homologs : (e + 1) * homologs, k * pair_ch : (k + 1) * pair_ch] = part[
                k * homologs : (k + 1) * homologs, :
            ]
    update = dot(right_ref[...], lw_scr[...]) * inv_ref[...]
    for k in range(lines):
        out_ref[k] = (update[:, k * pair_ch : (k + 1) * pair_ch] + offset_ref[...]).astype(BF16)


def msa_kernel(msa_ref, grads_ref, wf_ref, wl_ref, out_ref, scr):
    homologs, lines, depth = msa_ref.shape
    derivative = dot(grads_ref[0], wf_ref[...]) + dot(grads_ref[1], wl_ref[...])
    for h in range(depth // LANES):
        for k in range(lines):
            scr[h, pl.ds(k, homologs, stride=lines), :] = derivative[
                k * homologs : (k + 1) * homologs, h * LANES : (h + 1) * LANES
            ]
    derivative = jnp.concatenate([scr[h] for h in range(depth // LANES)], axis=1)
    normed, spread = normalize(msa_ref)
    one = jnp.mean(derivative, axis=-1, keepdims=True)
    two = jnp.mean(derivative * normed, axis=-1, keepdims=True)
    out = (derivative - one - normed * two) * spread
    out_ref[...] = out.reshape(homologs, lines, depth).astype(BF16)


def last_kernel(
    total, pos_ref, own_b_ref, other_b_ref, own_a_ref, other_a_ref,
    out_ref, former_ref, latter_ref, offset_ref,
):
    scale = 1.0 / total
    width = former_ref.shape[0]
    half = out_ref.shape[0] // PAIR
    early = own_a_ref.shape[0]
    late = half - early
    me = pos_ref[0] % PAIR
    for core, a_ref, b_ref in ((me, own_a_ref, own_b_ref), (1 - me, other_a_ref, other_b_ref)):
        at = core * half
        out_ref[pl.ds(pl.multiple_of(at, half), early), :] = a_ref[...].astype(F32) * scale
        out_ref[pl.ds(pl.multiple_of(at + early, width), late), :] = (
            b_ref[:late, :].astype(F32) * scale
        )
    parts = (own_b_ref[late:, :].astype(F32) + other_b_ref[late:, :].astype(F32)) * scale
    both = jnp.concatenate([parts[: 2 * width], parts[2 * width : 4 * width]], axis=1)
    former_ref[...] = both[:width]
    latter_ref[...] = both[width:]
    offset_ref[...] = parts[4 * width : 4 * width + 1]


def call(kernel, outs, scratch=(), smem=0, ins=0, flops=0, away=0, limit=VMEM_LIMIT):
    vmem = pl.BlockSpec(memory_space=pltpu.VMEM)
    return pl.pallas_call(
        kernel,
        out_shape=[jax.ShapeDtypeStruct(shape, kind) for shape, kind in outs],
        in_specs=[pl.BlockSpec(memory_space=pltpu.SMEM)] * smem
        + [pl.BlockSpec(memory_space=pltpu.HBM)] * away
        + [vmem] * ins,
        out_specs=[pl.BlockSpec(memory_space=pl.ANY) if away else vmem] * len(outs),
        scratch_shapes=[pltpu.VMEM(shape, kind) for shape, kind in scratch]
        + [pltpu.SemaphoreType.DMA((away + len(outs),))] * (away > 0),
        compiler_params=pltpu.CompilerParams(vmem_limit_bytes=limit),
        cost_estimate=pl.CostEstimate(flops=flops, bytes_accessed=0, transcendentals=0),
    )


def body(size, msa, mask, wf, wl, wout, offset, cot):
    homologs, lines, depth = msa.shape
    width = wf.shape[1]
    total, pair_ch = cot.shape[1:]
    wide = width * homologs
    rows = lines * homologs
    cols = lines * pair_ch
    span = 2 * wide + LANES + 2 * cols
    wf, wl = wf.T, wl.T
    pos = lax.axis_index(("chip", "core")).astype(jnp.int32).reshape(1)
    given = [msa, mask.T, wf, wl, cot]
    chips = size // 2
    left, right, maskb, low, *slots = call(
        pre_kernel,
        [
            ((rows, width), BF16),
            ((rows, width), BF16),
            ((homologs, lines * LANES), BF16),
            ((rows, depth), BF16),
        ]
        + [((lines, span), BF16)] * chips,
        [(x.shape, x.dtype) for x in given]
        + [
            ((depth // LANES, rows, LANES), F32),
            ((lines * total, pair_ch), F32),
            ((rows, width), BF16),
            ((rows, width), BF16),
            ((homologs, lines * LANES), BF16),
            ((rows, depth), BF16),
            ((chips, lines, span), BF16),
        ],
        smem=1,
        away=len(given),
        limit=None,
    )(pos, *given)

    def swap(x, step):
        return lax.ppermute(x, ("chip", "core"), [(i, i ^ step) for i in range(size)])

    def add(x, y):
        return (x.astype(F32) + y.astype(F32)).astype(BF16)

    offsets = sorted(range(chips), key=lambda m: (-(m // 4), -(m // 2), m))
    if chips <= DIRECT:
        near = [swap(slots[m], 2 * m) if m else slots[0] for m in offsets]
    else:
        order = (pos[0] // 2) ^ jnp.arange(chips)
        near = lax.all_to_all(jnp.stack(slots)[order], "chip", 0, 0)[order]
        near = [near[m] for m in offsets]
    far = [swap(slot, 1) for slot in near]
    other_right, other_maskb = swap(right, 1), swap(maskb, 1)
    (wleft,) = call(
        weight_kernel,
        [((width, width * pair_ch), BF16)],
        [((width * width, pair_ch), F32)],
        ins=1,
    )(wout)
    near, wleft = lax.optimization_barrier((near, wleft))
    half = width * width // PAIR
    early = half * 15 // 16
    sums, late, all_right, all_left, by_col, inv, own_p = call(
        functools.partial(half_kernel, offsets),
        [
            ((early, pair_ch), BF16),
            ((half - early, pair_ch), BF16),
            ((total, wide), BF16),
            ((total, wide), BF16),
            ((total, cols), BF16),
            ((total, cols), F32),
            ((rows, width * pair_ch // PAIR), BF16),
        ],
        [((size, lines, span), BF16), ((rows, width * pair_ch // PAIR), BF16)],
        smem=1,
        ins=4 + 2 * chips,
    )(pos, *near, *far, maskb, other_maskb, right, other_right)
    parts, grads = call(
        grads_kernel,
        [
            ((half - early + 4 * width + 16, pair_ch), BF16),
            ((2, rows, width), BF16),
        ],
        [((rows, width * pair_ch // PAIR), BF16), ((rows, width * pair_ch), BF16)],
        smem=1,
        ins=11,
    )(pos, own_p, all_right, all_left, by_col, inv, cot, wout, wleft, maskb, low, late)

    def make_update():
        (out,) = call(
            update_kernel,
            [((lines, total, pair_ch), BF16)],
            [((wide, cols), BF16)],
            ins=5,
            flops=2 * total * wide * cols,
        )(all_right, inv, left, wleft, offset.reshape(1, pair_ch))
        return out

    def make_d_msa():
        (out,) = call(
            msa_kernel,
            [((homologs, lines, depth), BF16)],
            [((depth // LANES, rows, LANES), F32)],
            ins=4,
            flops=2 * rows * depth * 2 * width,
        )(msa, grads, wf, wl)
        return out

    steps = [1 << n for n in range(1, size.bit_length() - 1)]
    work = [make_d_msa, make_update]
    done = []
    for step_a, step_b in zip(steps, steps[1:] + steps[:1]):
        sums = add(sums, swap(sums, step_a))
        got = swap(parts, step_b)
        if work:
            out = work.pop(0)()
            got, out = lax.optimization_barrier((got, out))
            done.append(out)
        parts = add(parts, got)
    d_msa, update = done
    d_out, d_former, d_latter, d_offset = call(
        functools.partial(last_kernel, total),
        [
            ((width * width, pair_ch), F32),
            ((width, depth), F32),
            ((width, depth), F32),
            ((1, pair_ch), F32),
        ],
        smem=1,
        ins=4,
    )(pos, parts, swap(parts, 1), sums, swap(sums, 1))
    return update, d_msa, d_former.T, d_latter.T, d_out, d_offset.reshape(pair_ch)


def solution(mesh):
    size = mesh.shape["row"]
    split = Mesh(mesh.devices.reshape(-1, size // 2, 2), ("grp", "chip", "core"))
    whole = ("grp", "chip", "core")
    return jax.shard_map(
        functools.partial(body, size),
        mesh=split,
        in_specs=(P(None, whole, None), P(None, whole), P(), P(), P(), P(), P(whole, None, None)),
        out_specs=(
            P(whole, None, None),
            P(None, whole, None),
            P("grp", None),
            P("grp", None),
            P("grp", None),
            P("grp"),
        ),
        check_vma=False,
    )
```

```python
import functools

import jax
import jax.numpy as jnp
from jax import lax
from jax.experimental import pallas as pl
from jax.experimental.pallas import tpu as pltpu
from jax.sharding import Mesh
from jax.sharding import PartitionSpec as P

F32 = jnp.float32
BF16 = jnp.bfloat16
LANES = 128
EPS = 1e-05
VMEM_LIMIT = 40 * 1024 * 1024
PAIR = 2
DIRECT = 8


def dot(a, b, ca=1, cb=0):
    return lax.dot_general(a, b, (((ca,), (cb,)), ((), ())), preferred_element_type=F32)


def normalize(msa_ref):
    homologs, lines, depth = msa_ref.shape
    x = msa_ref[...].astype(F32).reshape(homologs * lines, depth)
    centred = x - jnp.mean(x, axis=-1, keepdims=True)
    spread = lax.rsqrt(jnp.mean(centred * centred, axis=-1, keepdims=True) + EPS)
    return centred * spread, spread


def pre_kernel(
    pos_ref, msa_hbm, mask_hbm, wf_hbm, wl_hbm, cot_hbm,
    left_ref, right_ref, maskb_ref, low_ref, *refs
):
    slots, refs = refs[:-13], refs[-13:]
    msa_ref, mask_ref, wf_ref, wl_ref, cot_ref, norm_scr, cot_scr = refs[:7]
    left_scr, right_scr, maskb_scr, low_scr, slot_scr, sems = refs[7:]
    sent = []

    def send(source, target):
        sent.append(pltpu.make_async_copy(source, target, sems.at[len(copies) + len(sent)]))
        sent[-1].start()

    copies = [
        pltpu.make_async_copy(source, target, sems.at[n])
        for n, (source, target) in enumerate(
            [
                (msa_hbm, msa_ref),
                (wf_hbm, wf_ref),
                (wl_hbm, wl_ref),
                (mask_hbm, mask_ref),
                (cot_hbm, cot_ref),
            ]
        )
    ]
    for copy in copies:
        copy.start()
    homologs, lines, depth = msa_ref.shape
    width = wf_ref.shape[0]
    rows = homologs * lines
    wide = width * homologs
    total, pair_ch = cot_ref.shape[1:]
    chip, core = pos_ref[0] // 2, pos_ref[0] % 2
    copies[0].wait()
    normed, _ = normalize(msa_ref)
    for h in range(depth // LANES):
        norm_scr[h] = normed[:, h * LANES : (h + 1) * LANES]
    low = jnp.concatenate(
        [
            jnp.concatenate(
                [norm_scr[h, pl.ds(k, homologs, stride=lines), :] for k in range(lines)], axis=0
            )
            for h in range(depth // LANES)
        ],
        axis=1,
    ).astype(BF16)
    low_scr[...] = low
    send(low_scr, low_ref)
    for copy in copies[1:4]:
        copy.wait()
    mask = mask_ref[...].astype(F32).T
    cols = [jnp.broadcast_to(mask[:, k : k + 1], (homologs, LANES)) for k in range(lines)]
    for k in range(lines):
        maskb_scr[:, k * LANES : (k + 1) * LANES] = cols[k].astype(BF16)
    send(maskb_scr, maskb_ref)
    mask_rows = jnp.concatenate(cols, axis=0)
    weights = jnp.concatenate([wl_ref[...], wf_ref[...]], axis=0)
    both = (dot(low, weights, 1, 1) * mask_rows[:, : 2 * width]).astype(BF16)
    right, left = both[:, :width], both[:, width:]
    left_scr[...] = left
    right_scr[...] = right
    send(left_scr, left_ref)
    send(right_scr, right_ref)
    spread_to = (
        lax.broadcasted_iota(jnp.int32, (2 * width, 2 * wide), 1) // homologs
        == lax.broadcasted_iota(jnp.int32, (2 * width, 2 * wide), 0)
    ).astype(BF16)
    own_tile = (
        lax.broadcasted_iota(jnp.int32, (homologs, LANES), 1) % homologs
        == lax.broadcasted_iota(jnp.int32, (homologs, LANES), 0)
    ).astype(F32)
    own_rows = jnp.concatenate([own_tile] * lines, axis=0)
    own = jnp.concatenate([own_rows] * (2 * wide // LANES), axis=1)
    first = (lax.broadcasted_iota(jnp.int32, (rows, LANES), 1) < homologs).astype(F32)
    fold = (
        lax.broadcasted_iota(jnp.int32, (lines, rows), 1) // homologs
        == lax.broadcasted_iota(jnp.int32, (lines, rows), 0)
    ).astype(BF16)
    same = jnp.concatenate(
        [
            (dot(both, spread_to) * own).astype(BF16),
            (mask_rows * own_rows * first).astype(BF16),
        ],
        axis=1,
    )
    same = dot(fold, same).astype(BF16)
    base = same.shape[1]
    cols = lines * pair_ch
    copies[4].wait()
    cot_scr[...] = cot_ref[...].astype(F32).reshape(lines * total, pair_ch)
    for m, slot in enumerate(slots):
        slot_scr[m, :, cols : cols + base] = same
        for begin, to in ((0, core), (cols + base, 1 - core)):
            first = (2 * (chip ^ m) + to) * lines
            for k in range(lines):
                slot_scr[m, :, begin + k * pair_ch : begin + (k + 1) * pair_ch] = cot_scr[
                    pl.ds(first + k, lines, stride=total), :
                ].astype(BF16)
        send(slot_scr.at[m], slot)
    for copy in sent:
        copy.wait()


def weight_kernel(wout_ref, wleft_ref, w_scr):
    width, pair_ch = wleft_ref.shape[0], wout_ref.shape[1]
    w_scr[...] = wout_ref[...].astype(F32)
    for e in range(width):
        wleft_ref[:, e * pair_ch : (e + 1) * pair_ch] = w_scr[
            pl.ds(e, width, stride=width), :
        ].astype(BF16)


def half_kernel(offsets, pos_ref, *refs):
    early_ref, late_ref, right_ref, left_ref, by_col_ref, inv_ref, p_ref, got_scr, p_scr = refs[-9:]
    slots, (mask_a_ref, right_a_ref) = refs[:-11], refs[-11:-9]
    near, far = slots[: len(slots) // 2], slots[len(slots) // 2 :]
    rows, width = right_a_ref.shape
    homologs, cols = mask_a_ref.shape
    wide = width * homologs
    lines = rows // homologs
    pair_ch = cols // lines
    span = wide // PAIR
    base = cols + 2 * wide + LANES
    chip, core = pos_ref[0] // 2, pos_ref[0] % 2
    for m, a_ref, b_ref in zip(offsets, near, far):
        tile = 2 * (chip ^ m)
        got_scr[tile + core] = a_ref[...]
        got_scr[tile + 1 - core, :, cols:base] = b_ref[:, cols:base]
        got_scr[tile + 1 - core, :, :cols] = b_ref[:, base:]
        got_scr[tile + 1 - core, :, base:] = b_ref[:, :cols]

    def load(start, size):
        return got_scr[:, :, pl.ds(start, size)].astype(F32).reshape(-1, size)

    right_ref[...] = load(cols, wide).astype(BF16)
    left_ref[...] = load(cols + wide, wide).astype(BF16)
    left = left_ref[:, pl.ds(pl.multiple_of(core * span, span), span)]
    masks = load(cols + 2 * wide, LANES).astype(BF16)
    group = LANES // homologs
    mask_b = got_scr[2 * chip + 1 - core, :, cols + 2 * wide : base].astype(F32).T[:homologs]
    mask_b = jnp.concatenate(
        [jnp.broadcast_to(mask_b[:, k : k + 1], (homologs, LANES)) for k in range(lines)], axis=1
    ).astype(BF16)
    spread_to = (
        lax.broadcasted_iota(jnp.int32, (width, wide), 1) // homologs
        == lax.broadcasted_iota(jnp.int32, (width, wide), 0)
    ).astype(BF16)
    own_tile = (
        lax.broadcasted_iota(jnp.int32, (homologs, LANES), 1) % homologs
        == lax.broadcasted_iota(jnp.int32, (homologs, LANES), 0)
    ).astype(F32)
    own = jnp.concatenate([own_tile] * (wide // LANES), axis=1)
    right_b = got_scr[2 * chip + 1 - core, :, cols : cols + wide].astype(F32)
    right_b = jnp.concatenate(
        [jnp.broadcast_to(right_b[k : k + 1], (homologs, wide)) * own for k in range(lines)], axis=0
    ).astype(BF16)
    right_b = dot(right_b, spread_to, 1, 1).astype(BF16)
    sides = (mask_a_ref[...], right_a_ref[...], 0, p_ref), (mask_b, right_b, base, p_scr)
    out = 0.0
    for m, (mask, side, start, to_ref) in enumerate(sides):
        inv = 1.0 / (dot(masks[:, :homologs], mask) + 1.0)
        cot = (load(start, cols) * inv).astype(BF16)
        if m == 0:
            inv_ref[...] = inv
            by_col_ref[...] = cot
        for g in range(span // LANES):
            part = dot(left[:, g * LANES : (g + 1) * LANES], cot, 0, 0).astype(BF16)
            for b in range(group):
                c = g * group + b
                for k in range(lines):
                    to = k * homologs
                    to_ref[to : to + homologs, c * pair_ch : (c + 1) * pair_ch] = part[
                        b * homologs : (b + 1) * homologs, k * pair_ch : (k + 1) * pair_ch
                    ]
        out = out + dot(side, to_ref[...], 0, 0)
    out = out.astype(BF16)
    cut = early_ref.shape[0] // width
    for c in range(width // PAIR):
        line = out[:, c * pair_ch : (c + 1) * pair_ch]
        if c < cut:
            early_ref[c * width : (c + 1) * width, :] = line
        else:
            late_ref[(c - cut) * width : (c - cut + 1) * width, :] = line


def grads_kernel(
    pos_ref, p_ref, right_ref, left_ref, by_col_ref, inv_ref, cot_ref, wout_ref, wleft_ref, maskb_ref, low_ref, late_ref,
    parts_ref, grads_ref,
    p_scr, q_scr,
):
    lines, total, pair_ch = cot_ref.shape
    homologs = maskb_ref.shape[0]
    width = wleft_ref.shape[0]
    wide = width * homologs
    rows = lines * homologs
    bias = 0.0
    by_row = []
    for k in range(lines):
        line = cot_ref[k].astype(F32)
        bias = bias + jnp.sum(line, axis=0, keepdims=True)
        by_row.append((line * inv_ref[:, k * LANES : (k + 1) * LANES]).astype(BF16))
    by_row = jnp.concatenate(by_row, axis=1)
    group = LANES // homologs
    span = wide // PAIR
    core = pos_ref[0] % PAIR
    for out_ref, source, other in (
        (p_scr, left_ref[:, pl.ds(pl.multiple_of((1 - core) * span, span), span)], by_col_ref[...]),
        (q_scr, right_ref[...], by_row),
    ):
        for g in range(source.shape[1] // LANES):
            part = dot(source[:, g * LANES : (g + 1) * LANES], other, 0, 0).astype(BF16)
            for b in range(group):
                c = g * group + b
                for k in range(lines):
                    at = k * homologs
                    out_ref[at : at + homologs, c * pair_ch : (c + 1) * pair_ch] = part[
                        b * homologs : (b + 1) * homologs, k * pair_ch : (k + 1) * pair_ch
                    ]

    def weights(half):
        size = wout_ref.shape[0] // PAIR
        block = wout_ref[pl.ds(pl.multiple_of(half * size, size), size), :]
        return jnp.concatenate(
            [block[c * width : (c + 1) * width] for c in range(width // PAIR)], axis=1
        )

    mask_rows = jnp.concatenate(
        [maskb_ref[:, k * LANES : k * LANES + width] for k in range(lines)], axis=0
    ).astype(F32)
    right_sum = dot(p_ref[...], weights(core), 1, 1) + dot(p_scr[...], weights(1 - core), 1, 1)
    right_grad = (right_sum * mask_rows).astype(BF16)
    left_grad = (dot(q_scr[...], wleft_ref[...], 1, 1) * mask_rows).astype(BF16)
    grads_ref[0] = left_grad
    grads_ref[1] = right_grad
    part_left = dot(left_grad, low_ref[...], 0, 0)
    part_right = dot(right_grad, low_ref[...], 0, 0)
    begin = late_ref.shape[0]
    parts_ref[:begin, :] = late_ref[...]
    for h in range(2):
        lanes = slice(h * pair_ch, (h + 1) * pair_ch)
        at = begin + 2 * h * width
        parts_ref[at : at + width, :] = part_left[:, lanes].astype(BF16)
        parts_ref[at + width : at + 2 * width, :] = part_right[:, lanes].astype(BF16)
    at = begin + 4 * width
    parts_ref[at:, :] = jnp.broadcast_to(bias, (parts_ref.shape[0] - at, pair_ch)).astype(BF16)


def update_kernel(right_ref, inv_ref, left_ref, wleft_ref, offset_ref, out_ref, lw_scr):
    lines, total, pair_ch = out_ref.shape
    rows, width = left_ref.shape
    homologs = rows // lines
    for e in range(width):
        part = dot(left_ref[...], wleft_ref[:, e * pair_ch : (e + 1) * pair_ch]).astype(BF16)
        for k in range(lines):
            lw_scr[e * homologs : (e + 1) * homologs, k * pair_ch : (k + 1) * pair_ch] = part[
                k * homologs : (k + 1) * homologs, :
            ]
    update = dot(right_ref[...], lw_scr[...]) * inv_ref[...]
    for k in range(lines):
        out_ref[k] = (update[:, k * pair_ch : (k + 1) * pair_ch] + offset_ref[...]).astype(BF16)


def msa_kernel(msa_ref, grads_ref, wf_ref, wl_ref, out_ref, scr):
    homologs, lines, depth = msa_ref.shape
    derivative = dot(grads_ref[0], wf_ref[...]) + dot(grads_ref[1], wl_ref[...])
    for h in range(depth // LANES):
        for k in range(lines):
            scr[h, pl.ds(k, homologs, stride=lines), :] = derivative[
                k * homologs : (k + 1) * homologs, h * LANES : (h + 1) * LANES
            ]
    derivative = jnp.concatenate([scr[h] for h in range(depth // LANES)], axis=1)
    normed, spread = normalize(msa_ref)
    one = jnp.mean(derivative, axis=-1, keepdims=True)
    two = jnp.mean(derivative * normed, axis=-1, keepdims=True)
    out = (derivative - one - normed * two) * spread
    out_ref[...] = out.reshape(homologs, lines, depth).astype(BF16)


def last_kernel(
    total, pos_ref, own_b_ref, other_b_ref, own_a_ref, other_a_ref,
    out_ref, former_ref, latter_ref, offset_ref,
):
    scale = 1.0 / total
    width = former_ref.shape[0]
    half = out_ref.shape[0] // PAIR
    early = own_a_ref.shape[0]
    late = half - early
    me = pos_ref[0] % PAIR
    for core, a_ref, b_ref in ((me, own_a_ref, own_b_ref), (1 - me, other_a_ref, other_b_ref)):
        at = core * half
        out_ref[pl.ds(pl.multiple_of(at, half), early), :] = a_ref[...].astype(F32) * scale
        out_ref[pl.ds(pl.multiple_of(at + early, width), late), :] = (
            b_ref[:late, :].astype(F32) * scale
        )
    parts = (own_b_ref[late:, :].astype(F32) + other_b_ref[late:, :].astype(F32)) * scale
    both = jnp.concatenate([parts[: 2 * width], parts[2 * width : 4 * width]], axis=1)
    former_ref[...] = both[:width]
    latter_ref[...] = both[width:]
    offset_ref[...] = parts[4 * width : 4 * width + 1]


def call(kernel, outs, scratch=(), smem=0, ins=0, flops=0, away=0, limit=VMEM_LIMIT):
    vmem = pl.BlockSpec(memory_space=pltpu.VMEM)
    return pl.pallas_call(
        kernel,
        out_shape=[jax.ShapeDtypeStruct(shape, kind) for shape, kind in outs],
        in_specs=[pl.BlockSpec(memory_space=pltpu.SMEM)] * smem
        + [pl.BlockSpec(memory_space=pltpu.HBM)] * away
        + [vmem] * ins,
        out_specs=[pl.BlockSpec(memory_space=pl.ANY) if away else vmem] * len(outs),
        scratch_shapes=[pltpu.VMEM(shape, kind) for shape, kind in scratch]
        + [pltpu.SemaphoreType.DMA((away + len(outs),))] * (away > 0),
        compiler_params=pltpu.CompilerParams(vmem_limit_bytes=limit),
        cost_estimate=pl.CostEstimate(flops=flops, bytes_accessed=0, transcendentals=0),
    )


def body(size, msa, mask, wf, wl, wout, offset, cot):
    homologs, lines, depth = msa.shape
    width = wf.shape[1]
    total, pair_ch = cot.shape[1:]
    wide = width * homologs
    rows = lines * homologs
    cols = lines * pair_ch
    span = 2 * wide + LANES + 2 * cols
    wf, wl = wf.T, wl.T
    pos = lax.axis_index(("chip", "core")).astype(jnp.int32).reshape(1)
    given = [msa, mask.T, wf, wl, cot]
    chips = size // 2
    left, right, maskb, low, *slots = call(
        pre_kernel,
        [
            ((rows, width), BF16),
            ((rows, width), BF16),
            ((homologs, lines * LANES), BF16),
            ((rows, depth), BF16),
        ]
        + [((lines, span), BF16)] * chips,
        [(x.shape, x.dtype) for x in given]
        + [
            ((depth // LANES, rows, LANES), F32),
            ((lines * total, pair_ch), F32),
            ((rows, width), BF16),
            ((rows, width), BF16),
            ((homologs, lines * LANES), BF16),
            ((rows, depth), BF16),
            ((chips, lines, span), BF16),
        ],
        smem=1,
        away=len(given),
        limit=None,
    )(pos, *given)

    def swap(x, step):
        return lax.ppermute(x, ("chip", "core"), [(i, i ^ step) for i in range(size)])

    def add(x, y):
        return (x.astype(F32) + y.astype(F32)).astype(BF16)

    offsets = sorted(range(chips), key=lambda m: (-(m // 4), -(m // 2), m))
    if chips <= DIRECT:
        near = [swap(slots[m], 2 * m) if m else slots[0] for m in offsets]
    else:
        order = (pos[0] // 2) ^ jnp.arange(chips)
        near = lax.all_to_all(jnp.stack(slots)[order], "chip", 0, 0)[order]
        near = [near[m] for m in offsets]
    far = [swap(slot, 1) for slot in near]
    (wleft,) = call(
        weight_kernel,
        [((width, width * pair_ch), BF16)],
        [((width * width, pair_ch), F32)],
        ins=1,
    )(wout)
    near, wleft = lax.optimization_barrier((near, wleft))
    half = width * width // PAIR
    early = half * 15 // 16
    sums, late, all_right, all_left, by_col, inv, own_p = call(
        functools.partial(half_kernel, offsets),
        [
            ((early, pair_ch), BF16),
            ((half - early, pair_ch), BF16),
            ((total, wide), BF16),
            ((total, wide), BF16),
            ((total, cols), BF16),
            ((total, cols), F32),
            ((rows, width * pair_ch // PAIR), BF16),
        ],
        [((size, lines, span), BF16), ((rows, width * pair_ch // PAIR), BF16)],
        smem=1,
        ins=2 + 2 * chips,
    )(pos, *near, *far, maskb, right)
    parts, grads = call(
        grads_kernel,
        [
            ((half - early + 4 * width + 16, pair_ch), BF16),
            ((2, rows, width), BF16),
        ],
        [((rows, width * pair_ch // PAIR), BF16), ((rows, width * pair_ch), BF16)],
        smem=1,
        ins=11,
    )(pos, own_p, all_right, all_left, by_col, inv, cot, wout, wleft, maskb, low, late)

    def make_update():
        (out,) = call(
            update_kernel,
            [((lines, total, pair_ch), BF16)],
            [((wide, cols), BF16)],
            ins=5,
            flops=2 * total * wide * cols,
        )(all_right, inv, left, wleft, offset.reshape(1, pair_ch))
        return out

    def make_d_msa():
        (out,) = call(
            msa_kernel,
            [((homologs, lines, depth), BF16)],
            [((depth // LANES, rows, LANES), F32)],
            ins=4,
            flops=2 * rows * depth * 2 * width,
        )(msa, grads, wf, wl)
        return out

    steps = [1 << n for n in range(1, size.bit_length() - 1)]
    work = [make_d_msa, make_update]
    done = []
    for step_a, step_b in zip(steps, steps[1:] + steps[:1]):
        sums = add(sums, swap(sums, step_a))
        got = swap(parts, step_b)
        if work:
            out = work.pop(0)()
            got, out = lax.optimization_barrier((got, out))
            done.append(out)
        parts = add(parts, got)
    d_msa, update = done
    d_out, d_former, d_latter, d_offset = call(
        functools.partial(last_kernel, total),
        [
            ((width * width, pair_ch), F32),
            ((width, depth), F32),
            ((width, depth), F32),
            ((1, pair_ch), F32),
        ],
        smem=1,
        ins=4,
    )(pos, parts, swap(parts, 1), sums, swap(sums, 1))
    return update, d_msa, d_former.T, d_latter.T, d_out, d_offset.reshape(pair_ch)


def solution(mesh):
    size = mesh.shape["row"]
    split = Mesh(mesh.devices.reshape(-1, size // 2, 2), ("grp", "chip", "core"))
    whole = ("grp", "chip", "core")
    return jax.shard_map(
        functools.partial(body, size),
        mesh=split,
        in_specs=(P(None, whole, None), P(None, whole), P(), P(), P(), P(), P(whole, None, None)),
        out_specs=(
            P(whole, None, None),
            P(None, whole, None),
            P("grp", None),
            P("grp", None),
            P("grp", None),
            P("grp"),
        ),
        check_vma=False,
    )
```

```python
import functools

import jax
import jax.numpy as jnp
from jax import lax
from jax.experimental import pallas as pl
from jax.experimental.pallas import tpu as pltpu
from jax.sharding import Mesh
from jax.sharding import PartitionSpec as P

F32 = jnp.float32
BF16 = jnp.bfloat16
LANES = 128
EPS = 1e-05
VMEM_LIMIT = 40 * 1024 * 1024
PAIR = 2
DIRECT = 8


def dot(a, b, ca=1, cb=0):
    return lax.dot_general(a, b, (((ca,), (cb,)), ((), ())), preferred_element_type=F32)


def normalize(msa_ref):
    homologs, lines, depth = msa_ref.shape
    x = msa_ref[...].astype(F32).reshape(homologs * lines, depth)
    centred = x - jnp.mean(x, axis=-1, keepdims=True)
    spread = lax.rsqrt(jnp.mean(centred * centred, axis=-1, keepdims=True) + EPS)
    return centred * spread, spread


def pre_kernel(
    pos_ref, msa_hbm, mask_hbm, wf_hbm, wl_hbm, cot_hbm,
    left_ref, right_ref, maskb_ref, low_ref, *refs
):
    slots, refs = refs[:-13], refs[-13:]
    msa_ref, mask_ref, wf_ref, wl_ref, cot_ref, norm_scr, cot_scr = refs[:7]
    left_scr, right_scr, maskb_scr, low_scr, slot_scr, sems = refs[7:]
    sent = []

    def send(source, target):
        sent.append(pltpu.make_async_copy(source, target, sems.at[len(copies) + len(sent)]))
        sent[-1].start()

    copies = [
        pltpu.make_async_copy(source, target, sems.at[n])
        for n, (source, target) in enumerate(
            [
                (msa_hbm, msa_ref),
                (wf_hbm, wf_ref),
                (wl_hbm, wl_ref),
                (mask_hbm, mask_ref),
                (cot_hbm, cot_ref),
            ]
        )
    ]
    for copy in copies:
        copy.start()
    homologs, lines, depth = msa_ref.shape
    width = wf_ref.shape[0]
    rows = homologs * lines
    wide = width * homologs
    total, pair_ch = cot_ref.shape[1:]
    chip, core = pos_ref[0] // 2, pos_ref[0] % 2
    copies[0].wait()
    normed, _ = normalize(msa_ref)
    for h in range(depth // LANES):
        norm_scr[h, :rows] = normed[:, h * LANES : (h + 1) * LANES]
    low = jnp.concatenate(
        [
            jnp.concatenate(
                [norm_scr[h, pl.ds(k, homologs, stride=lines), :] for k in range(lines)], axis=0
            )
            for h in range(depth // LANES)
        ],
        axis=1,
    ).astype(BF16)
    low_scr[...] = low
    send(low_scr, low_ref)
    for copy in copies[1:4]:
        copy.wait()
    mask = mask_ref[...].astype(F32).T
    cols = [jnp.broadcast_to(mask[:, k : k + 1], (homologs, LANES)) for k in range(lines)]
    for k in range(lines):
        maskb_scr[:, k * LANES : (k + 1) * LANES] = cols[k].astype(BF16)
    send(maskb_scr, maskb_ref)
    mask_rows = jnp.concatenate(cols, axis=0)
    weights = jnp.concatenate([wl_ref[...], wf_ref[...]], axis=0)
    both = (dot(low, weights, 1, 1) * mask_rows[:, : 2 * width]).astype(BF16)
    right, left = both[:, :width], both[:, width:]
    left_scr[...] = left
    right_scr[...] = right
    send(left_scr, left_ref)
    send(right_scr, right_ref)
    spread_to = (
        lax.broadcasted_iota(jnp.int32, (2 * width, 2 * wide), 1) // homologs
        == lax.broadcasted_iota(jnp.int32, (2 * width, 2 * wide), 0)
    ).astype(BF16)
    own_tile = (
        lax.broadcasted_iota(jnp.int32, (homologs, LANES), 1) % homologs
        == lax.broadcasted_iota(jnp.int32, (homologs, LANES), 0)
    ).astype(F32)
    own_rows = jnp.concatenate([own_tile] * lines, axis=0)
    own = jnp.concatenate([own_rows] * (2 * wide // LANES), axis=1)
    first = (lax.broadcasted_iota(jnp.int32, (rows, LANES), 1) < homologs).astype(F32)
    fold = (
        lax.broadcasted_iota(jnp.int32, (lines, rows), 1) // homologs
        == lax.broadcasted_iota(jnp.int32, (lines, rows), 0)
    ).astype(BF16)
    same = jnp.concatenate(
        [
            (dot(both, spread_to) * own).astype(BF16),
            (mask_rows * own_rows * first).astype(BF16),
        ],
        axis=1,
    )
    same = dot(fold, same).astype(BF16)
    base = same.shape[1]
    cols = lines * pair_ch
    copies[4].wait()
    cot_scr[: lines * total] = cot_ref[...].astype(F32).reshape(lines * total, pair_ch)
    for m, slot in enumerate(slots):
        slot_scr[m, :, cols : cols + base] = same
        for begin, to in ((0, core), (cols + base, 1 - core)):
            first = (2 * (chip ^ m) + to) * lines
            for k in range(lines):
                slot_scr[m, :, begin + k * pair_ch : begin + (k + 1) * pair_ch] = cot_scr[
                    pl.ds(first + k, lines, stride=total), :
                ].astype(BF16)
        send(slot_scr.at[m], slot)
    for copy in sent:
        copy.wait()


def weight_kernel(wout_ref, wleft_ref, w_scr):
    width, pair_ch = wleft_ref.shape[0], wout_ref.shape[1]
    w_scr[: wout_ref.shape[0]] = wout_ref[...].astype(F32)
    for e in range(width):
        wleft_ref[:, e * pair_ch : (e + 1) * pair_ch] = w_scr[
            pl.ds(e, width, stride=width), :
        ].astype(BF16)


def half_kernel(offsets, pos_ref, *refs):
    early_ref, late_ref, right_ref, left_ref, by_col_ref, inv_ref, p_ref, got_scr, p_scr = refs[-9:]
    slots, (mask_a_ref, right_a_ref) = refs[:-11], refs[-11:-9]
    near, far = slots[: len(slots) // 2], slots[len(slots) // 2 :]
    rows, width = right_a_ref.shape
    homologs, cols = mask_a_ref.shape
    wide = width * homologs
    lines = rows // homologs
    pair_ch = cols // lines
    span = wide // PAIR
    base = cols + 2 * wide + LANES
    chip, core = pos_ref[0] // 2, pos_ref[0] % 2
    for m, a_ref, b_ref in zip(offsets, near, far):
        tile = 2 * (chip ^ m)
        got_scr[tile + core] = a_ref[...]
        got_scr[tile + 1 - core, :, cols:base] = b_ref[:, cols:base]
        got_scr[tile + 1 - core, :, :cols] = b_ref[:, base:]
        got_scr[tile + 1 - core, :, base:] = b_ref[:, :cols]

    def load(start, size):
        return got_scr[:, :, pl.ds(start, size)].astype(F32).reshape(-1, size)

    right_ref[...] = load(cols, wide).astype(BF16)
    left_ref[...] = load(cols + wide, wide).astype(BF16)
    left = left_ref[:, pl.ds(pl.multiple_of(core * span, span), span)]
    masks = load(cols + 2 * wide, LANES).astype(BF16)
    group = LANES // homologs
    mask_b = got_scr[2 * chip + 1 - core, :, cols + 2 * wide : base].astype(F32).T[:homologs]
    mask_b = jnp.concatenate(
        [jnp.broadcast_to(mask_b[:, k : k + 1], (homologs, LANES)) for k in range(lines)], axis=1
    ).astype(BF16)
    spread_to = (
        lax.broadcasted_iota(jnp.int32, (width, wide), 1) // homologs
        == lax.broadcasted_iota(jnp.int32, (width, wide), 0)
    ).astype(BF16)
    own_tile = (
        lax.broadcasted_iota(jnp.int32, (homologs, LANES), 1) % homologs
        == lax.broadcasted_iota(jnp.int32, (homologs, LANES), 0)
    ).astype(F32)
    own = jnp.concatenate([own_tile] * (wide // LANES), axis=1)
    right_b = got_scr[2 * chip + 1 - core, :, cols : cols + wide].astype(F32)
    right_b = jnp.concatenate(
        [jnp.broadcast_to(right_b[k : k + 1], (homologs, wide)) * own for k in range(lines)], axis=0
    ).astype(BF16)
    right_b = dot(right_b, spread_to, 1, 1).astype(BF16)
    sides = (mask_a_ref[...], right_a_ref[...], 0, p_ref), (mask_b, right_b, base, p_scr)
    out = 0.0
    for m, (mask, side, start, to_ref) in enumerate(sides):
        inv = 1.0 / (dot(masks[:, :homologs], mask) + 1.0)
        cot = (load(start, cols) * inv).astype(BF16)
        if m == 0:
            inv_ref[...] = inv
            by_col_ref[...] = cot
        for g in range(span // LANES):
            part = dot(left[:, g * LANES : (g + 1) * LANES], cot, 0, 0).astype(BF16)
            for b in range(group):
                c = g * group + b
                for k in range(lines):
                    to = k * homologs
                    to_ref[to : to + homologs, c * pair_ch : (c + 1) * pair_ch] = part[
                        b * homologs : (b + 1) * homologs, k * pair_ch : (k + 1) * pair_ch
                    ]
        out = out + dot(side, to_ref[...], 0, 0)
    out = out.astype(BF16)
    cut = early_ref.shape[0] // width
    for c in range(width // PAIR):
        line = out[:, c * pair_ch : (c + 1) * pair_ch]
        if c < cut:
            early_ref[c * width : (c + 1) * width, :] = line
        else:
            late_ref[(c - cut) * width : (c - cut + 1) * width, :] = line


def grads_kernel(
    pos_ref, p_ref, right_ref, left_ref, by_col_ref, inv_ref, cot_ref, wout_ref, wleft_ref, maskb_ref, low_ref, late_ref,
    parts_ref, grads_ref,
    p_scr, q_scr,
):
    lines, total, pair_ch = cot_ref.shape
    homologs = maskb_ref.shape[0]
    width = wleft_ref.shape[0]
    wide = width * homologs
    rows = lines * homologs
    bias = 0.0
    by_row = []
    for k in range(lines):
        line = cot_ref[k].astype(F32)
        bias = bias + jnp.sum(line, axis=0, keepdims=True)
        by_row.append((line * inv_ref[:, k * LANES : (k + 1) * LANES]).astype(BF16))
    by_row = jnp.concatenate(by_row, axis=1)
    group = LANES // homologs
    span = wide // PAIR
    core = pos_ref[0] % PAIR
    for out_ref, source, other in (
        (p_scr, left_ref[:, pl.ds(pl.multiple_of((1 - core) * span, span), span)], by_col_ref[...]),
        (q_scr, right_ref[...], by_row),
    ):
        for g in range(source.shape[1] // LANES):
            part = dot(source[:, g * LANES : (g + 1) * LANES], other, 0, 0).astype(BF16)
            for b in range(group):
                c = g * group + b
                for k in range(lines):
                    at = k * homologs
                    out_ref[at : at + homologs, c * pair_ch : (c + 1) * pair_ch] = part[
                        b * homologs : (b + 1) * homologs, k * pair_ch : (k + 1) * pair_ch
                    ]

    def weights(half):
        size = wout_ref.shape[0] // PAIR
        block = wout_ref[pl.ds(pl.multiple_of(half * size, size), size), :]
        return jnp.concatenate(
            [block[c * width : (c + 1) * width] for c in range(width // PAIR)], axis=1
        )

    mask_rows = jnp.concatenate(
        [maskb_ref[:, k * LANES : k * LANES + width] for k in range(lines)], axis=0
    ).astype(F32)
    right_sum = dot(p_ref[...], weights(core), 1, 1) + dot(p_scr[...], weights(1 - core), 1, 1)
    right_grad = (right_sum * mask_rows).astype(BF16)
    left_grad = (dot(q_scr[...], wleft_ref[...], 1, 1) * mask_rows).astype(BF16)
    grads_ref[0] = left_grad
    grads_ref[1] = right_grad
    part_left = dot(left_grad, low_ref[...], 0, 0)
    part_right = dot(right_grad, low_ref[...], 0, 0)
    begin = late_ref.shape[0]
    parts_ref[:begin, :] = late_ref[...]
    for h in range(2):
        lanes = slice(h * pair_ch, (h + 1) * pair_ch)
        at = begin + 2 * h * width
        parts_ref[at : at + width, :] = part_left[:, lanes].astype(BF16)
        parts_ref[at + width : at + 2 * width, :] = part_right[:, lanes].astype(BF16)
    at = begin + 4 * width
    parts_ref[at:, :] = jnp.broadcast_to(bias, (parts_ref.shape[0] - at, pair_ch)).astype(BF16)


def update_kernel(right_ref, inv_ref, left_ref, wleft_ref, offset_ref, out_ref, lw_scr):
    lines, total, pair_ch = out_ref.shape
    rows, width = left_ref.shape
    homologs = rows // lines
    for e in range(width):
        part = dot(left_ref[...], wleft_ref[:, e * pair_ch : (e + 1) * pair_ch]).astype(BF16)
        for k in range(lines):
            lw_scr[e * homologs : (e + 1) * homologs, k * pair_ch : (k + 1) * pair_ch] = part[
                k * homologs : (k + 1) * homologs, :
            ]
    update = dot(right_ref[...], lw_scr[...]) * inv_ref[...]
    for k in range(lines):
        out_ref[k] = (update[:, k * pair_ch : (k + 1) * pair_ch] + offset_ref[...]).astype(BF16)


def msa_kernel(msa_ref, grads_ref, wf_ref, wl_ref, out_ref, scr):
    homologs, lines, depth = msa_ref.shape
    derivative = dot(grads_ref[0], wf_ref[...]) + dot(grads_ref[1], wl_ref[...])
    for h in range(depth // LANES):
        for k in range(lines):
            scr[h, pl.ds(k, homologs, stride=lines), :] = derivative[
                k * homologs : (k + 1) * homologs, h * LANES : (h + 1) * LANES
            ]
    derivative = jnp.concatenate(
        [scr[h, : homologs * lines] for h in range(depth // LANES)], axis=1
    )
    normed, spread = normalize(msa_ref)
    one = jnp.mean(derivative, axis=-1, keepdims=True)
    two = jnp.mean(derivative * normed, axis=-1, keepdims=True)
    out = (derivative - one - normed * two) * spread
    out_ref[...] = out.reshape(homologs, lines, depth).astype(BF16)


def last_kernel(
    total, pos_ref, own_b_ref, other_b_ref, own_a_ref, other_a_ref,
    out_ref, former_ref, latter_ref, offset_ref,
):
    scale = 1.0 / total
    width = former_ref.shape[0]
    half = out_ref.shape[0] // PAIR
    early = own_a_ref.shape[0]
    late = half - early
    me = pos_ref[0] % PAIR
    for core, a_ref, b_ref in ((me, own_a_ref, own_b_ref), (1 - me, other_a_ref, other_b_ref)):
        at = core * half
        out_ref[pl.ds(pl.multiple_of(at, half), early), :] = a_ref[...].astype(F32) * scale
        out_ref[pl.ds(pl.multiple_of(at + early, width), late), :] = (
            b_ref[:late, :].astype(F32) * scale
        )
    parts = (own_b_ref[late:, :].astype(F32) + other_b_ref[late:, :].astype(F32)) * scale
    both = jnp.concatenate([parts[: 2 * width], parts[2 * width : 4 * width]], axis=1)
    former_ref[...] = both[:width]
    latter_ref[...] = both[width:]
    offset_ref[...] = parts[4 * width : 4 * width + 1]


def call(kernel, outs, scratch=(), smem=0, ins=0, flops=0, away=0, limit=VMEM_LIMIT):
    vmem = pl.BlockSpec(memory_space=pltpu.VMEM)
    return pl.pallas_call(
        kernel,
        out_shape=[jax.ShapeDtypeStruct(shape, kind) for shape, kind in outs],
        in_specs=[pl.BlockSpec(memory_space=pltpu.SMEM)] * smem
        + [pl.BlockSpec(memory_space=pltpu.HBM)] * away
        + [vmem] * ins,
        out_specs=[pl.BlockSpec(memory_space=pl.ANY) if away else vmem] * len(outs),
        scratch_shapes=[pltpu.VMEM(shape, kind) for shape, kind in scratch]
        + [pltpu.SemaphoreType.DMA((away + len(outs),))] * (away > 0),
        compiler_params=pltpu.CompilerParams(vmem_limit_bytes=limit),
        cost_estimate=pl.CostEstimate(flops=flops, bytes_accessed=0, transcendentals=0),
    )


def body(size, msa, mask, wf, wl, wout, offset, cot):
    homologs, lines, depth = msa.shape
    width = wf.shape[1]
    total, pair_ch = cot.shape[1:]
    wide = width * homologs
    rows = lines * homologs
    cols = lines * pair_ch
    span = 2 * wide + LANES + 2 * cols
    wf, wl = wf.T, wl.T
    pos = lax.axis_index(("chip", "core")).astype(jnp.int32).reshape(1)
    given = [msa, mask.T, wf, wl, cot]
    chips = size // 2
    left, right, maskb, low, *slots = call(
        pre_kernel,
        [
            ((rows, width), BF16),
            ((rows, width), BF16),
            ((homologs, lines * LANES), BF16),
            ((rows, depth), BF16),
        ]
        + [((lines, span), BF16)] * chips,
        [(x.shape, x.dtype) for x in given]
        + [
            ((depth // LANES, rows + lines, LANES), F32),
            (((lines + 1) * total, pair_ch), F32),
            ((rows, width), BF16),
            ((rows, width), BF16),
            ((homologs, lines * LANES), BF16),
            ((rows, depth), BF16),
            ((chips, lines, span), BF16),
        ],
        smem=1,
        away=len(given),
        limit=None,
    )(pos, *given)

    def swap(x, step):
        return lax.ppermute(x, ("chip", "core"), [(i, i ^ step) for i in range(size)])

    def add(x, y):
        return (x.astype(F32) + y.astype(F32)).astype(BF16)

    offsets = sorted(range(chips), key=lambda m: (-(m // 4), -(m // 2), m))
    if chips <= DIRECT:
        near = [swap(slots[m], 2 * m) if m else slots[0] for m in offsets]
    else:
        order = (pos[0] // 2) ^ jnp.arange(chips)
        near = lax.all_to_all(jnp.stack(slots)[order], "chip", 0, 0)[order]
        near = [near[m] for m in offsets]
    far = [swap(slot, 1) for slot in near]
    (wleft,) = call(
        weight_kernel,
        [((width, width * pair_ch), BF16)],
        [((width * width + width, pair_ch), F32)],
        ins=1,
    )(wout)
    near, wleft = lax.optimization_barrier((near, wleft))
    half = width * width // PAIR
    early = half * 15 // 16
    sums, late, all_right, all_left, by_col, inv, own_p = call(
        functools.partial(half_kernel, offsets),
        [
            ((early, pair_ch), BF16),
            ((half - early, pair_ch), BF16),
            ((total, wide), BF16),
            ((total, wide), BF16),
            ((total, cols), BF16),
            ((total, cols), F32),
            ((rows, width * pair_ch // PAIR), BF16),
        ],
        [((size, lines, span), BF16), ((rows, width * pair_ch // PAIR), BF16)],
        smem=1,
        ins=2 + 2 * chips,
    )(pos, *near, *far, maskb, right)
    parts, grads = call(
        grads_kernel,
        [
            ((half - early + 4 * width + 16, pair_ch), BF16),
            ((2, rows, width), BF16),
        ],
        [((rows, width * pair_ch // PAIR), BF16), ((rows, width * pair_ch), BF16)],
        smem=1,
        ins=11,
    )(pos, own_p, all_right, all_left, by_col, inv, cot, wout, wleft, maskb, low, late)

    def make_update():
        (out,) = call(
            update_kernel,
            [((lines, total, pair_ch), BF16)],
            [((wide, cols), BF16)],
            ins=5,
            flops=2 * total * wide * cols,
        )(all_right, inv, left, wleft, offset.reshape(1, pair_ch))
        return out

    def make_d_msa():
        (out,) = call(
            msa_kernel,
            [((homologs, lines, depth), BF16)],
            [((depth // LANES, rows + lines, LANES), F32)],
            ins=4,
            flops=2 * rows * depth * 2 * width,
        )(msa, grads, wf, wl)
        return out

    steps = [1 << n for n in range(1, size.bit_length() - 1)]
    work = [make_d_msa, make_update]
    done = []
    for step_a, step_b in zip(steps, steps[1:] + steps[:1]):
        sums = add(sums, swap(sums, step_a))
        got = swap(parts, step_b)
        if work:
            out = work.pop(0)()
            got, out = lax.optimization_barrier((got, out))
            done.append(out)
        parts = add(parts, got)
    d_msa, update = done
    d_out, d_former, d_latter, d_offset = call(
        functools.partial(last_kernel, total),
        [
            ((width * width, pair_ch), F32),
            ((width, depth), F32),
            ((width, depth), F32),
            ((1, pair_ch), F32),
        ],
        smem=1,
        ins=4,
    )(pos, parts, swap(parts, 1), sums, swap(sums, 1))
    return update, d_msa, d_former.T, d_latter.T, d_out, d_offset.reshape(pair_ch)


def solution(mesh):
    size = mesh.shape["row"]
    split = Mesh(mesh.devices.reshape(-1, size // 2, 2), ("grp", "chip", "core"))
    whole = ("grp", "chip", "core")
    return jax.shard_map(
        functools.partial(body, size),
        mesh=split,
        in_specs=(P(None, whole, None), P(None, whole), P(), P(), P(), P(), P(whole, None, None)),
        out_specs=(
            P(whole, None, None),
            P(None, whole, None),
            P("grp", None),
            P("grp", None),
            P("grp", None),
            P("grp"),
        ),
        check_vma=False,
    )
```
